32 devices in a mesh: rep: 2 (over y), exp: 8 (over z, x), dec: 2 (over core).
Axes of the slice: x: 2, y: 2, z: 4, core: 2. Of those that a mesh axis runs over, the one named last changes fastest.
Arguments:
- tokens: bfloat16 [4096, 1024], P(('rep', 'exp', 'dec')), parts along dimension 0, may hold values from -6 to 6
- expert_ids: int32 [4096, 2], P(('rep', 'exp', 'dec')), parts along dimension 0, may hold values from 0 to 3, as said below
- gate_logits: float32 [4096, 2], P(('rep', 'exp', 'dec')), parts along dimension 0, may hold values from -4.25 to 4.25
- source_lengths: int32 [32], P(('rep', 'exp', 'dec')), parts along dimension 0, may hold values from 96 to 128
- page_table: int32 [32], P(('rep', 'exp', 'dec')), parts along dimension 0, may hold values from 0 to 1, as said below
- norm_gain: float32 [1024], replicated, may hold values from 0.1 to 1.9
- final_gain: float32 [1024], replicated, may hold values from 0.1 to 1.9
- w_in: bfloat16 [8, 1024, 2048], P('exp', None, 'dec'), may hold values from -0.1875 to 0.1875
- w_out: bfloat16 [8, 2048, 1024], P('exp', 'dec'), may hold values from -0.09375 to 0.09375
- w_kv: bfloat16 [1024, 2048], P(('exp', 'dec')), may hold values from -0.1875 to 0.1875
- b_kv: float32 [2048], replicated, may hold values from -3 to 3
Outputs:
- kv_pages: bfloat16 [32, 128, 2048], P(('rep', 'exp', 'dec')), parts along dimension 0
The draws below stay inside these ranges and needn't reach their ends.
There are 2 independent parts, one for each index of `rep`. The reference program is written for one: setup_inputs(seed, part) draws one part's arguments, and reference() takes and returns one part's arrays. A program takes and returns all parts, laid end to end along the dimension named above; an argument that names none is the same for every part. Nothing has to cross between parts.
Inputs may be any that keep to these rules, and one draw needn't show every extreme that they name: `expert_ids`: each row names two different experts; within the rows of one device (aligned blocks of 128 rows) one expert is named exactly 96 times, all on rows before that page's length, and every other expert at most (162) // 3 times. `page_table`: pages 2 c and 2 c + 1 always go to different cores.
All inputs are finite; a program needn't handle non-finite values.
Results may differ from the reference program's by a relative error of at most 0.0053.
Values may be sent and summed in bfloat16 or wider, within the bound.
A program may use at most 64 MiB of HBM per device.

```python
import jax
import jax.numpy as jnp
from jax import lax

D = 1024
FF = 4096
PAGE = 128
TOK_DEV = 128
EXPERTS = 4
CAP = 96
KV_COLS = 2048
PAGES = 16
TOKENS = 2048


def shared_lengths(key):
    key = jax.random.fold_in(key, 5)
    key_one, key_two, key_three, key_four = jax.random.split(key, 4)
    reach = PAGE - CAP + 1
    first = jax.random.randint(key_one, (PAGES,), 0, reach).astype(jnp.int32)
    second = jax.random.randint(key_two, (PAGES,), 0, reach).astype(jnp.int32)
    lengths = PAGE - first * second // reach
    long_page = jax.random.randint(key_three, (), 0, PAGES).astype(jnp.int32)
    short_page = (long_page + 1 + jax.random.randint(key_four, (), 0, PAGES - 1).astype(jnp.int32)) % PAGES
    index = jnp.arange(PAGES, dtype=jnp.int32)
    lengths = jnp.where(index == long_page, PAGE, lengths)
    lengths = jnp.where(index == short_page, CAP, lengths)
    return lengths.astype(jnp.int32)


def draw_source_lengths(key, part):
    return shared_lengths(key)


def draw_expert_ids(key, part):
    lengths = shared_lengths(key)
    key = jax.random.fold_in(key, 13)
    key_hot, key_rest = jax.random.split(key, 2)
    hot_order = jax.random.permutation(key_hot, EXPERTS).astype(jnp.int32)
    block_keys = jax.random.split(key_rest, PAGES)
    others_count = EXPERTS - 1

    def one_block(block_key, length):
        keys = jax.random.split(block_key, 7)
        first = jax.random.randint(keys[0], (), 0, EXPERTS).astype(jnp.int32)
        second = jax.random.randint(keys[1], (), 0, EXPERTS).astype(jnp.int32)
        crowded = hot_order[first * second // EXPERTS]
        rows = jnp.arange(TOK_DEV, dtype=jnp.int32)
        noise = jax.random.randint(keys[2], (TOK_DEV,), 0, 1 << 16).astype(jnp.int32)
        score = noise * TOK_DEV + rows + jnp.where(rows < length, 0, 1 << 30).astype(jnp.int32)
        order = jnp.argsort(score)
        rank = jnp.zeros((TOK_DEV,), jnp.int32).at[order].set(rows)
        holds = rank < CAP
        hot_slot = jax.random.randint(keys[3], (TOK_DEV,), 0, 2).astype(jnp.int32)
        shuffle_score = jax.random.randint(keys[4], (TOK_DEV,), 0, 1 << 16).astype(jnp.int32) * TOK_DEV + rows
        row_order = jnp.argsort(shuffle_score)
        needs = jnp.where(holds, 1, 2).astype(jnp.int32)
        needs_sorted = needs[row_order]
        start_sorted = jnp.cumsum(needs_sorted) - needs_sorted
        start = jnp.zeros((TOK_DEV,), jnp.int32).at[row_order].set(start_sorted.astype(jnp.int32))
        offset = jax.random.randint(keys[5], (), 0, others_count).astype(jnp.int32)
        mixing = jax.random.permutation(keys[6], EXPERTS).astype(jnp.int32)
        place = jnp.sum(jnp.arange(EXPERTS, dtype=jnp.int32) * (mixing == crowded).astype(jnp.int32))
        slots = jnp.arange(others_count, dtype=jnp.int32)
        others = mixing[slots + (slots >= place).astype(jnp.int32)]
        first_other = others[(start + offset) % others_count]
        second_other = others[(start + 1 + offset) % others_count]
        column_zero = jnp.where(holds, jnp.where(hot_slot == 0, crowded, first_other), first_other)
        column_one = jnp.where(holds, jnp.where(hot_slot == 0, first_other, crowded), second_other)
        return jnp.stack([column_zero, column_one], axis=1)
    chosen = jax.vmap(one_block)(block_keys, lengths)
    return chosen.reshape(TOKENS, 2).astype(jnp.int32)


def draw_gate_logits(key, part):
    key = jax.random.fold_in(key, 17)
    key_level, key_gap = jax.random.split(key, 2)
    level = jnp.clip(1.5 * jax.random.normal(key_level, (TOKENS, 1), jnp.float32), -4.0, 4.0)
    gap = jnp.clip(0.12 * jax.random.normal(key_gap, (TOKENS, 1), jnp.float32), -0.25, 0.25)
    return jnp.concatenate([level + gap, level - gap], axis=1).astype(jnp.float32)


def draw_page_table(key, part):
    key = jax.random.fold_in(key, 11)
    chip_flips = jax.random.randint(key, (PAGES // 2,), 0, 2).astype(jnp.int32)
    core_index = jnp.arange(PAGES, dtype=jnp.int32) % 2
    return (core_index ^ jnp.repeat(chip_flips, 2)).astype(jnp.int32)


def level_of(rng, extent, cuts, least, top_value):
    def one(axis_at, shards_of):
        heights = jax.random.uniform(jax.random.fold_in(jax.random.fold_in(rng, 6), axis_at), (shards_of,), jnp.float32, least / len(cuts), top_value / len(cuts))
        return jnp.repeat(jnp.exp(heights), extent[axis_at] // shards_of).reshape((-1,) + (1,) * (len(extent) - axis_at - 1))

    loudness = one(*cuts[0])
    for cut in cuts[1:]:
        loudness = loudness * one(*cut)
    return loudness


def bell_draw(rng, extent, scale, most, cuts=(), kind=jnp.bfloat16):
    entries = jax.random.normal(rng, extent, jnp.float32) * scale
    if len(cuts) > 0:
        entries = level_of(rng, extent, cuts, -0.22, 0.18) * entries
    return jnp.clip(entries, min=-most, max=most).astype(kind)


def setup_inputs(seed: int = 0, part: int = 0) -> dict:
    arg_keys = jax.random.split(jax.random.key(seed), 12)
    part_splits = jax.random.split(jax.random.fold_in(arg_keys[11], part), 12)
    return {
        "tokens": bell_draw(part_splits[0], (TOKENS, D), 1.0, 6.0, ((0, 16),)),
        "expert_ids": draw_expert_ids(jax.random.fold_in(jax.random.fold_in(arg_keys[11], part), 71), part),
        "gate_logits": draw_gate_logits(jax.random.fold_in(jax.random.fold_in(arg_keys[11], part), 71), part),
        "source_lengths": draw_source_lengths(jax.random.fold_in(jax.random.fold_in(arg_keys[11], part), 71), part),
        "page_table": draw_page_table(jax.random.fold_in(jax.random.fold_in(arg_keys[11], part), 71), part),
        "norm_gain": jnp.clip(1.0 + 0.18 * jax.random.normal(arg_keys[5], (D,), jnp.float32), 0.1, 1.9),
        "final_gain": jnp.clip(1.0 + 0.18 * jax.random.normal(arg_keys[6], (D,), jnp.float32), 0.1, 1.9),
        "w_in": bell_draw(arg_keys[7], (2 * EXPERTS, D, FF // 2), D ** -0.5, 0.1875, ((0, 8), (2, 2))),
        "w_out": bell_draw(arg_keys[8], (2 * EXPERTS, FF // 2, D), FF ** -0.5, 0.09375, ((0, 8), (1, 2))),
        "w_kv": bell_draw(arg_keys[9], (D, KV_COLS), D ** -0.5, 0.1875, ((0, 16),)),
        "b_kv": bell_draw(arg_keys[10], (KV_COLS,), 0.5, 3.0, (), jnp.float32),
    }


epsilon = 1e-05

def layer_norm(values, scale_gain):
    values = values.astype(jnp.float32)
    center = values - lax.optimization_barrier(jnp.mean(values, axis=-1, keepdims=True))
    spread = lax.optimization_barrier(jnp.mean(center * center, axis=-1, keepdims=True))
    return center * lax.rsqrt(spread + epsilon) * scale_gain

def reference(tokens, expert_ids, gate_logits, source_lengths, page_table, norm_gain, final_gain, w_in, w_out, w_kv, b_kv):
    position = jnp.arange(TOKENS, dtype=jnp.int32)
    is_valid = position % PAGE < jnp.repeat(source_lengths, PAGE)
    normed = layer_norm(tokens, norm_gain).astype(jnp.bfloat16)
    pair_ids = expert_ids.reshape(-1)
    pair_live = jnp.repeat(is_valid, 2)
    onehot = ((pair_ids[:, None] == jnp.arange(EXPERTS, dtype=jnp.int32)[None, :]) & pair_live[:, None]).astype(jnp.int32)
    blocks = onehot.reshape(-1, 2 * TOK_DEV, EXPERTS)
    pair_slots = lax.optimization_barrier(jnp.sum((jnp.cumsum(blocks, axis=1) - blocks) * blocks, axis=2)).reshape(-1)
    sources = TOKENS // TOK_DEV
    source = jnp.repeat(jnp.arange(sources, dtype=jnp.int32), 2 * TOK_DEV)
    row_of = source * CAP + pair_slots
    spread_rows = sources * CAP
    inputs = jnp.repeat(normed, 2, axis=0)

    def one_expert(outputs, expert_index):
        chosen = pair_live & (pair_ids == expert_index)
        target = jnp.where(chosen, row_of, spread_rows)
        buffer = jnp.zeros((spread_rows, D), jnp.bfloat16).at[target].set(inputs, mode='drop')
        w_inner = jnp.concatenate([w_in[2 * expert_index], w_in[2 * expert_index + 1]], axis=1)
        w_outer = jnp.concatenate([w_out[2 * expert_index], w_out[2 * expert_index + 1]], axis=0)
        hidden = jnp.maximum(jnp.dot(buffer, w_inner, preferred_element_type=jnp.float32), 0.0).astype(jnp.bfloat16)
        result = jnp.dot(hidden, w_outer, preferred_element_type=jnp.float32).astype(jnp.bfloat16)
        taken_rows = result[jnp.minimum(target, spread_rows - 1)]
        return (jnp.where(chosen[:, None], taken_rows, outputs), None)
    outputs, _ = lax.scan(one_expert, jnp.zeros((2 * TOKENS, D), jnp.bfloat16), jnp.arange(EXPERTS, dtype=jnp.int32))
    gate_weights = jax.nn.sigmoid(gate_logits - gate_logits[:, ::-1])
    picked = outputs.astype(jnp.float32).reshape(TOKENS, 2, D)
    mixed_out = lax.optimization_barrier(jnp.sum(gate_weights[:, :, None] * picked, axis=1))
    residual_sum = tokens.astype(jnp.float32) + jnp.where(is_valid[:, None], mixed_out, 0.0)
    encoded = layer_norm(residual_sum, final_gain).astype(jnp.bfloat16)
    projected = jnp.dot(encoded, w_kv, preferred_element_type=jnp.float32) + b_kv
    keys_values = jnp.where(is_valid[:, None], projected, 0.0).astype(jnp.bfloat16).reshape(PAGES, PAGE, KV_COLS)
    owner_slot = 2 * (jnp.arange(PAGES, dtype=jnp.int32) // 2) + page_table
    return jnp.zeros_like(keys_values).at[owner_slot].set(keys_values)
```

```python
import functools

import jax
import jax.numpy as jnp
from jax import lax
from jax.experimental import pallas as pl
from jax.experimental.pallas import tpu as pltpu
from jax.sharding import PartitionSpec as P

epsilon = 1e-05
MESH = pl.DeviceIdType.MESH


def partner(value, axis, bit):
    mask = 2**bit
    pairs = [(source, source ^ mask) for source in range(lax.axis_size(axis))]
    return lax.ppermute(value, axis, pairs)


def layer_norm(values, scale_gain):
    values = values.astype(jnp.float32)
    center = values - jnp.mean(values, axis=-1, keepdims=True)
    spread = jnp.mean(center * center, axis=-1, keepdims=True)
    return center * lax.rsqrt(spread + epsilon) * scale_gain


def route_slots(expert_ids, is_valid, experts):
    pair_ids = expert_ids.reshape(-1)
    pair_live = jnp.repeat(is_valid, 2)
    onehot = (
        (pair_ids[:, None] == jnp.arange(experts, dtype=jnp.int32)[None, :]) & pair_live[:, None]
    ).astype(jnp.int32)
    before = jnp.cumsum(onehot, axis=0) - onehot
    pair_slots = jnp.sum(before * onehot, axis=1)
    return (pair_ids, pair_live, pair_slots)


def shards(
    tokens,
    expert_ids,
    gate_logits,
    source_lengths,
    page_table,
    norm_gain,
    final_gain,
    w_in,
    w_out,
    w_kv,
    b_kv,
):
    tok_rows, feature_width = tokens.shape
    experts = lax.axis_size("exp") // 2
    capacity = 2 * max(1, (3 * tok_rows + experts - 1) // (2 * experts))
    half_cap = capacity // 2
    position = jnp.arange(tok_rows, dtype=jnp.int32)
    is_valid = position < source_lengths[0]
    normed = layer_norm(tokens, norm_gain).astype(jnp.bfloat16)
    pair_ids, pair_live, pair_slots = route_slots(expert_ids, is_valid, experts)
    overflow_row = experts * capacity
    target = jnp.where(pair_live, pair_ids * capacity + pair_slots, overflow_row)
    outgoing = (
        jnp.zeros((overflow_row, feature_width), jnp.bfloat16)
        .at[target]
        .set(jnp.repeat(normed, 2, axis=0), mode="drop")
    )
    arrived = lax.all_to_all(
        outgoing.reshape(2 * experts, half_cap, feature_width),
        "exp",
        split_axis=0,
        concat_axis=0,
        tiled=True,
    )
    partner_in, partner_out = partner((w_in, w_out), "exp", 0)
    w_inner = jnp.concatenate([w_in[0], partner_in[0]], axis=1)
    w_outer = jnp.concatenate([w_out[0], partner_out[0]], axis=0)
    local_rows = arrived[None]
    block_piece = lax.all_gather(local_rows[None], "dec", axis=0, tiled=True)
    flat_rows = block_piece.reshape(-1, feature_width)
    hidden = jnp.maximum(
        jnp.dot(flat_rows, w_inner, preferred_element_type=jnp.float32), 0.0
    ).astype(jnp.bfloat16)
    partial_out = jnp.dot(hidden, w_outer, preferred_element_type=jnp.float32).reshape(
        block_piece.shape
    )
    summed = partial_out[:, 0]
    reduced = lax.psum_scatter(summed, "dec", scatter_dimension=0, tiled=True)[0].astype(
        jnp.bfloat16
    )
    returned = lax.all_to_all(reduced, "exp", split_axis=0, concat_axis=0, tiled=True).reshape(
        overflow_row, feature_width
    )
    picked = (
        returned[jnp.minimum(target, overflow_row - 1)]
        .astype(jnp.float32)
        .reshape(tok_rows, 2, feature_width)
    )
    gate_weights = jax.nn.sigmoid(gate_logits - gate_logits[:, ::-1])
    mixed_out = jnp.sum(gate_weights[:, :, None] * picked, axis=1)
    residual_sum = tokens.astype(jnp.float32) + jnp.where(is_valid[:, None], mixed_out, 0.0)
    encoded = layer_norm(residual_sum, final_gain).astype(jnp.bfloat16)
    my_core = lax.axis_index("dec")
    keep_own = page_table[0] == my_core
    page_length = source_lengths[0]
    projected = jnp.dot(
        encoded,
        lax.all_gather(w_kv, ("exp", "dec"), axis=0, tiled=True),
        preferred_element_type=jnp.float32,
    )
    keys_values = jnp.where((position < page_length)[:, None], projected + b_kv, 0.0).astype(
        jnp.bfloat16
    )
    page_result = jnp.where(keep_own, keys_values, partner(keys_values, "dec", 0))
    return page_result[None]


def fused_kernel(
    experts,
    capacity,
    tokens_ref,
    ids_ref,
    logits_ref,
    length_ref,
    page_ref,
    norm_ref,
    final_ref,
    w_in_ref,
    w_out_ref,
    enc_ref,
    live_ref,
    wi,
    wo,
    pick,
    sends,
    held,
    hid,
    own_sum,
    part_send,
    part_recv,
    back_send,
    back,
    swap_send,
    swap_recv,
    wl_sem,
    ws_sem,
    wr_sem,
    zs_sem,
    zr_sem,
    xs_sem,
    xr_sem,
    ps_sem,
    pr_sem,
    bs_sem,
    br_sem,
    es_sem,
    er_sem,
):
    rows, width = tokens_ref.shape
    group = lax.axis_index("exp")
    core = lax.axis_index("dec")
    z = group // 2
    side = group % 2
    across = 2 * z + (1 - side)

    def peer(step):
        return lax.rem(z + step, experts)

    def source(step):
        return lax.rem(z + experts - step, experts)

    barrier = pltpu.get_barrier_semaphore()
    pl.semaphore_signal(barrier, inc=1, device_id={"dec": 1 - core}, device_id_type=MESH)
    pl.semaphore_signal(barrier, inc=1, device_id={"exp": across}, device_id_type=MESH)
    for step in range(1, experts):
        pl.semaphore_signal(
            barrier, inc=1, device_id={"exp": 2 * peer(step) + side}, device_id_type=MESH
        )

    local_weights = [
        pltpu.make_async_copy(w_in_ref.at[0], wi.at[0], wl_sem.at[0]),
        pltpu.make_async_copy(w_out_ref.at[0], wo.at[0], wl_sem.at[1]),
    ]
    for copy in local_weights:
        copy.start()

    normed = layer_norm(tokens_ref[...], norm_ref[...]).astype(jnp.bfloat16)
    ids = ids_ref[...]
    live = lax.broadcasted_iota(jnp.int32, (rows, 1), 0) < length_ref[...]
    lane = lax.broadcasted_iota(jnp.int32, (rows, 128), 1)
    named = ((ids[:, 0:1] == lane) | (ids[:, 1:2] == lane)) & live
    earlier = lax.broadcasted_iota(jnp.int32, (rows, rows), 1) < lax.broadcasted_iota(
        jnp.int32, (rows, rows), 0
    )
    count = jnp.dot(
        earlier.astype(jnp.float32).astype(jnp.bfloat16),
        named.astype(jnp.float32).astype(jnp.bfloat16),
        preferred_element_type=jnp.float32,
    ).astype(jnp.int32)
    slots = jnp.where(named, count, -1)
    slot_lane = lax.broadcasted_iota(jnp.int32, (rows, capacity), 1)
    for e in range(experts):
        chosen = (slots[:, e : e + 1] == slot_lane).astype(jnp.float32).astype(jnp.bfloat16)
        pick[e] = chosen
        sends[e] = lax.dot_general(
            chosen, normed, (((0,), (0,)), ((), ())), preferred_element_type=jnp.float32
        ).astype(jnp.bfloat16)

    pl.semaphore_wait(barrier, experts + 1)

    def remote(src, dst, send_sem, recv_sem, where):
        return pltpu.make_async_remote_copy(
            src_ref=src,
            dst_ref=dst,
            send_sem=send_sem,
            recv_sem=recv_sem,
            device_id=where,
            device_id_type=MESH,
        )

    dispatch = []
    for step in range(1, experts):
        to = peer(step)
        copy = remote(
            sends.at[to],
            held.at[0, z],
            zs_sem.at[step],
            zr_sem.at[step],
            {"exp": 2 * to + side},
        )
        copy.start()
        dispatch.append(copy)
    held[0, z] = sends[z]

    swap_weights = [
        remote(w_in_ref.at[0], wi.at[1], ws_sem.at[0], wr_sem.at[0], {"dec": 1 - core}),
        remote(w_out_ref.at[0], wo.at[1], ws_sem.at[1], wr_sem.at[1], {"dec": 1 - core}),
    ]

    def forward(step):
        at = source(step)
        copy = remote(
            held.at[0, at], held.at[1, at], xs_sem.at[step], xr_sem.at[step], {"exp": across}
        )
        copy.start()
        return copy

    def part_copy(step):
        return remote(
            part_send.at[step],
            part_recv.at[step],
            ps_sem.at[step],
            pr_sem.at[step],
            {"exp": across},
        )

    def back_copy(step):
        return remote(
            back_send.at[step],
            back.at[z],
            bs_sem.at[step],
            br_sem.at[step],
            {"exp": 2 * source(step) + side},
        )

    unit = wi.shape[2]
    tile = 512

    def ffn(column, at, store):
        def inner(i, carry):
            half = i // (unit // tile)
            offset = pl.multiple_of(i % (unit // tile) * tile, tile)
            block = jnp.dot(
                held[column, at],
                wi[half, :, pl.ds(offset, tile)],
                preferred_element_type=jnp.float32,
            )
            hid[half, :, pl.ds(offset, tile)] = jnp.maximum(block, 0.0).astype(jnp.bfloat16)
            return carry

        lax.fori_loop(0, 2 * (unit // tile), inner, 0)

        def outer(i, carry):
            cols = pl.ds(pl.multiple_of(i * tile, tile), tile)
            total = jnp.dot(hid[0], wo[0, :, cols], preferred_element_type=jnp.float32)
            total += jnp.dot(hid[1], wo[1, :, cols], preferred_element_type=jnp.float32)
            store(cols, total)
            return carry

        lax.fori_loop(0, width // tile, outer, 0)

    def ffn_own(step):
        def store(cols, total):
            own_sum[step, :, cols] = total

        ffn(0, source(step), store)

    def ffn_other(step):
        def store(cols, total):
            part_send[step, :, cols] = total.astype(jnp.bfloat16)

        ffn(1, source(step), store)
        part_copy(step).start()

    def finish(step):
        part_copy(step).wait_recv()
        total = (own_sum[step] + part_recv[step].astype(jnp.float32)).astype(jnp.bfloat16)
        if step == 0:
            back[z] = total
        else:
            back_send[step] = total
            back_copy(step).start()

    forwards = [forward(0)]
    for copy in swap_weights:
        copy.start()
    for copy in local_weights:
        copy.wait()
    for copy in swap_weights:
        copy.wait_recv()
    ffn_own(0)
    for step in range(1, experts):
        dispatch[step - 1].wait_recv()
        forwards.append(forward(step))
        forwards[step - 1].wait_recv()
        ffn_other(step - 1)
        ffn_own(step)
        if step >= 2:
            finish(step - 2)
    forwards[experts - 1].wait_recv()
    ffn_other(experts - 1)
    finish(experts - 2)
    finish(experts - 1)

    logits = logits_ref[...]
    gates = jax.nn.sigmoid(logits[:, 0:1] - logits[:, 1:2])
    gates_other = jax.nn.sigmoid(logits[:, 1:2] - logits[:, 0:1])
    residual = tokens_ref[...].astype(jnp.float32)
    for step in range(experts):
        if step > 0:
            back_copy(step).wait_recv()
        e = peer(step)
        gate = jnp.where(ids[:, 0:1] == e, gates, gates_other)
        residual += gate * jnp.dot(pick[e], back[e], preferred_element_type=jnp.float32)
    encoded = layer_norm(residual, final_ref[...]).astype(jnp.bfloat16)
    mask = jnp.broadcast_to(live, (rows, 128)).astype(jnp.float32).astype(jnp.bfloat16)
    swap_send[:, :width] = encoded
    swap_send[:, width:] = mask
    exchange = remote(swap_send, swap_recv, es_sem, er_sem, {"dec": 1 - core})
    exchange.start()

    for copy in swap_weights + dispatch + forwards:
        copy.wait_send()
    for step in range(experts):
        part_copy(step).wait_send()
        if step > 0:
            back_copy(step).wait_send()
    exchange.wait()
    keep = page_ref[...] == core
    mine = swap_send[...].astype(jnp.float32)
    other = swap_recv[...].astype(jnp.float32)
    final = jnp.where(keep, mine, other).astype(jnp.bfloat16)
    enc_ref[...] = final[:, :width]
    live_ref[...] = final[:, width:]


def fused(
    capacity,
    tokens,
    expert_ids,
    gate_logits,
    source_lengths,
    page_table,
    norm_gain,
    final_gain,
    w_in,
    w_out,
):
    rows, width = tokens.shape
    unit = w_in.shape[2]
    experts = lax.axis_size("exp") // 2
    bf16 = jnp.bfloat16
    block = (experts, capacity, width)
    dma = pltpu.SemaphoreType.DMA
    vmem = pl.BlockSpec(memory_space=pltpu.VMEM)
    anywhere = pl.BlockSpec(memory_space=pl.ANY)
    return pl.pallas_call(
        functools.partial(fused_kernel, experts, capacity),
        out_shape=(
            jax.ShapeDtypeStruct((rows, width), bf16),
            jax.ShapeDtypeStruct((rows, 128), bf16),
        ),
        in_specs=[vmem] * 7 + [anywhere] * 2,
        out_specs=(vmem, vmem),
        scratch_shapes=[
            pltpu.VMEM((2,) + w_in.shape[1:], bf16),
            pltpu.VMEM((2,) + w_out.shape[1:], bf16),
            pltpu.VMEM((experts, rows, capacity), bf16),
            pltpu.VMEM(block, bf16),
            pltpu.VMEM((2,) + block, bf16),
            pltpu.VMEM((2, capacity, unit), bf16),
            pltpu.VMEM(block, jnp.float32),
            pltpu.VMEM(block, bf16),
            pltpu.VMEM(block, bf16),
            pltpu.VMEM(block, bf16),
            pltpu.VMEM(block, bf16),
            pltpu.VMEM((rows, width + 128), bf16),
            pltpu.VMEM((rows, width + 128), bf16),
            dma((2,)),
            dma((2,)),
            dma((2,)),
        ]
        + [dma((experts,)) for _ in range(8)]
        + [dma, dma],
        compiler_params=pltpu.CompilerParams(
            collective_id=0, has_side_effects=True, vmem_limit_bytes=40 * 1024 * 1024
        ),
        cost_estimate=pl.CostEstimate(
            flops=8 * experts * capacity * width * unit * 2,
            bytes_accessed=64 * 1024 * 1024,
            transcendentals=0,
        ),
        name="expert_layer",
    )(
        tokens,
        expert_ids,
        gate_logits,
        source_lengths.reshape(1, 1),
        page_table.reshape(1, 1),
        norm_gain.reshape(1, width),
        final_gain.reshape(1, width),
        w_in,
        w_out,
    )


def kernel_shards(capacity, *args):
    tokens, ids, logits, lengths, pages, norm_gain, final_gain, w_in, w_out, w_kv, b_kv = args
    w_full = lax.all_gather(w_kv, ("exp", "dec"), axis=0, tiled=True)
    encoded, live = fused(
        capacity, tokens, ids, logits, lengths, pages, norm_gain, final_gain, w_in, w_out
    )
    projected = jnp.dot(encoded, w_full, preferred_element_type=jnp.float32)
    keys_values = jnp.where(live[:, 0:1] > 0, projected + b_kv, 0.0).astype(jnp.bfloat16)
    return keys_values[None]


def any_shards(*args):
    tok_rows = args[0].shape[0]
    experts = lax.axis_size("exp") // 2
    capacity = 2 * max(1, (3 * tok_rows + experts - 1) // (2 * experts))
    if capacity % 16 == 0 and experts <= 8 and lax.axis_size("dec") == 2:
        return kernel_shards(capacity, *args)
    return shards(*args)


def solution(mesh):
    return jax.shard_map(
        any_shards,
        mesh=mesh,
        in_specs=(
            P(("rep", "exp", "dec"), None),
            P(("rep", "exp", "dec"), None),
            P(("rep", "exp", "dec"), None),
            P(("rep", "exp", "dec")),
            P(("rep", "exp", "dec")),
            P(),
            P(),
            P("exp", None, "dec"),
            P("exp", "dec", None),
            P(("exp", "dec"), None),
            P(),
        ),
        out_specs=P(("rep", "exp", "dec"), None, None),
        check_vma=False,
    )
```

```python
import functools

import jax
import jax.numpy as jnp
from jax import lax
from jax.experimental import pallas as pl
from jax.experimental.pallas import tpu as pltpu
from jax.sharding import PartitionSpec as P

epsilon = 1e-05
MESH = pl.DeviceIdType.MESH


def partner(value, axis, bit):
    mask = 2**bit
    pairs = [(source, source ^ mask) for source in range(lax.axis_size(axis))]
    return lax.ppermute(value, axis, pairs)


def layer_norm(values, scale_gain):
    values = values.astype(jnp.float32)
    center = values - jnp.mean(values, axis=-1, keepdims=True)
    spread = jnp.mean(center * center, axis=-1, keepdims=True)
    return center * lax.rsqrt(spread + epsilon) * scale_gain


def route_slots(expert_ids, is_valid, experts):
    pair_ids = expert_ids.reshape(-1)
    pair_live = jnp.repeat(is_valid, 2)
    onehot = (
        (pair_ids[:, None] == jnp.arange(experts, dtype=jnp.int32)[None, :]) & pair_live[:, None]
    ).astype(jnp.int32)
    before = jnp.cumsum(onehot, axis=0) - onehot
    pair_slots = jnp.sum(before * onehot, axis=1)
    return (pair_ids, pair_live, pair_slots)


def shards(
    tokens,
    expert_ids,
    gate_logits,
    source_lengths,
    page_table,
    norm_gain,
    final_gain,
    w_in,
    w_out,
    w_kv,
    b_kv,
):
    tok_rows, feature_width = tokens.shape
    experts = lax.axis_size("exp") // 2
    capacity = 2 * max(1, (3 * tok_rows + experts - 1) // (2 * experts))
    half_cap = capacity // 2
    position = jnp.arange(tok_rows, dtype=jnp.int32)
    is_valid = position < source_lengths[0]
    normed = layer_norm(tokens, norm_gain).astype(jnp.bfloat16)
    pair_ids, pair_live, pair_slots = route_slots(expert_ids, is_valid, experts)
    overflow_row = experts * capacity
    target = jnp.where(pair_live, pair_ids * capacity + pair_slots, overflow_row)
    outgoing = (
        jnp.zeros((overflow_row, feature_width), jnp.bfloat16)
        .at[target]
        .set(jnp.repeat(normed, 2, axis=0), mode="drop")
    )
    arrived = lax.all_to_all(
        outgoing.reshape(2 * experts, half_cap, feature_width),
        "exp",
        split_axis=0,
        concat_axis=0,
        tiled=True,
    )
    partner_in, partner_out = partner((w_in, w_out), "exp", 0)
    w_inner = jnp.concatenate([w_in[0], partner_in[0]], axis=1)
    w_outer = jnp.concatenate([w_out[0], partner_out[0]], axis=0)
    local_rows = arrived[None]
    block_piece = lax.all_gather(local_rows[None], "dec", axis=0, tiled=True)
    flat_rows = block_piece.reshape(-1, feature_width)
    hidden = jnp.maximum(
        jnp.dot(flat_rows, w_inner, preferred_element_type=jnp.float32), 0.0
    ).astype(jnp.bfloat16)
    partial_out = jnp.dot(hidden, w_outer, preferred_element_type=jnp.float32).reshape(
        block_piece.shape
    )
    summed = partial_out[:, 0]
    reduced = lax.psum_scatter(summed, "dec", scatter_dimension=0, tiled=True)[0].astype(
        jnp.bfloat16
    )
    returned = lax.all_to_all(reduced, "exp", split_axis=0, concat_axis=0, tiled=True).reshape(
        overflow_row, feature_width
    )
    picked = (
        returned[jnp.minimum(target, overflow_row - 1)]
        .astype(jnp.float32)
        .reshape(tok_rows, 2, feature_width)
    )
    gate_weights = jax.nn.sigmoid(gate_logits - gate_logits[:, ::-1])
    mixed_out = jnp.sum(gate_weights[:, :, None] * picked, axis=1)
    residual_sum = tokens.astype(jnp.float32) + jnp.where(is_valid[:, None], mixed_out, 0.0)
    encoded = layer_norm(residual_sum, final_gain).astype(jnp.bfloat16)
    my_core = lax.axis_index("dec")
    keep_own = page_table[0] == my_core
    page_length = source_lengths[0]
    projected = jnp.dot(
        encoded,
        lax.all_gather(w_kv, ("exp", "dec"), axis=0, tiled=True),
        preferred_element_type=jnp.float32,
    )
    keys_values = jnp.where((position < page_length)[:, None], projected + b_kv, 0.0).astype(
        jnp.bfloat16
    )
    page_result = jnp.where(keep_own, keys_values, partner(keys_values, "dec", 0))
    return page_result[None]


def fused_kernel(
    experts,
    capacity,
    tokens_ref,
    ids_ref,
    logits_ref,
    length_ref,
    page_ref,
    norm_ref,
    final_ref,
    w_in_ref,
    w_out_ref,
    w_kv_ref,
    b_kv_ref,
    kv_ref,
    tok,
    ids_t,
    logits_t,
    norm,
    final,
    bias,
    kv,
    wk,
    wi,
    wo,
    pick,
    sends,
    held,
    hid,
    own_sum,
    part_send,
    part_recv,
    back_send,
    back,
    swap_send,
    swap_recv,
    wl_sem,
    ws_sem,
    wr_sem,
    zs_sem,
    zr_sem,
    xs_sem,
    xr_sem,
    ps_sem,
    pr_sem,
    bs_sem,
    br_sem,
    es_sem,
    er_sem,
    in_sem,
    kl_sem,
    zks_sem,
    zkr_sem,
    zls_sem,
    zlr_sem,
    xks_sem,
    xkr_sem,
    yks_sem,
    ykr_sem,
    dks_sem,
    dkr_sem,
    kv_sem,
):
    rows, width = tokens_ref.shape
    group = lax.axis_index("exp")
    part = lax.axis_index("rep")
    core = lax.axis_index("dec")
    z = group // 2
    side = group % 2
    across = 2 * z + (1 - side)

    def peer(step):
        other, bit = 0, 1
        while bit < experts:
            mine, flip = (z // bit) % 2, (step // bit) % 2
            other = other + bit * (mine + flip - 2 * mine * flip)
            bit *= 2
        return other

    inputs = [
        pltpu.make_async_copy(src, dst, in_sem.at[i])
        for i, (src, dst) in enumerate(
            (
                (tokens_ref, tok),
                (ids_ref, ids_t),
                (logits_ref, logits_t),
                (norm_ref, norm),
                (final_ref, final),
                (b_kv_ref, bias),
            )
        )
    ]
    for copy in inputs:
        copy.start()

    barrier = pltpu.get_barrier_semaphore()
    pl.semaphore_signal(barrier, inc=1, device_id={"dec": 1 - core}, device_id_type=MESH)
    pl.semaphore_signal(barrier, inc=1, device_id={"exp": across}, device_id_type=MESH)
    pl.semaphore_signal(barrier, inc=1, device_id={"rep": 1 - part}, device_id_type=MESH)
    for step in range(1, experts):
        pl.semaphore_signal(
            barrier, inc=1, device_id={"exp": 2 * peer(step) + side}, device_id_type=MESH
        )

    local_weights = [
        pltpu.make_async_copy(w_in_ref.at[0], wi.at[0], wl_sem.at[0]),
        pltpu.make_async_copy(w_out_ref.at[0], wo.at[0], wl_sem.at[1]),
    ]
    for copy in local_weights:
        copy.start()

    for copy in inputs:
        copy.wait()
    normed = layer_norm(tok[...], norm[...]).astype(jnp.bfloat16)
    row = lax.broadcasted_iota(jnp.int32, (rows, rows), 0)
    column = lax.broadcasted_iota(jnp.int32, (rows, rows), 1)

    def upright(line):
        return jnp.sum(jnp.where(row == column, line, 0.0), axis=1, keepdims=True)

    ids_f = ids_t[...].astype(jnp.float32)
    first, second = (upright(ids_f[k : k + 1]).astype(jnp.int32) for k in range(2))
    live = lax.broadcasted_iota(jnp.int32, (rows, 1), 0) < length_ref[0]
    lane = lax.broadcasted_iota(jnp.int32, (rows, 128), 1)
    named = ((first == lane) | (second == lane)) & live
    earlier = column < row
    count = jnp.dot(
        earlier.astype(jnp.float32).astype(jnp.bfloat16),
        named.astype(jnp.float32).astype(jnp.bfloat16),
        preferred_element_type=jnp.float32,
    ).astype(jnp.int32)
    slots = jnp.where(named, count, -1)
    slot_lane = lax.broadcasted_iota(jnp.int32, (rows, capacity), 1)
    for e in range(experts):
        chosen = (slots[:, e : e + 1] == slot_lane).astype(jnp.float32).astype(jnp.bfloat16)
        pick[e] = chosen
        sends[e] = lax.dot_general(
            chosen, normed, (((0,), (0,)), ((), ())), preferred_element_type=jnp.float32
        ).astype(jnp.bfloat16)

    pl.semaphore_wait(barrier, experts + 2)

    def remote(src, dst, send_sem, recv_sem, where):
        return pltpu.make_async_remote_copy(
            src_ref=src,
            dst_ref=dst,
            send_sem=send_sem,
            recv_sem=recv_sem,
            device_id=where,
            device_id_type=MESH,
        )

    def dispatch(step):
        to = peer(step)
        return remote(
            sends.at[to],
            held.at[0, z],
            zs_sem.at[step],
            zr_sem.at[step],
            {"exp": 2 * to + side},
        )

    block_rows = w_kv_ref.shape[0]
    half_rows = block_rows // 2

    def block(at, column_side, half):
        start = ((2 * at + column_side) * 2 + core) * block_rows + half * half_rows
        return wk.at[pl.ds(pl.multiple_of(start, half_rows), half_rows)]

    own_start = pl.multiple_of((2 * group + core) * block_rows, block_rows)
    own_block = wk.at[pl.ds(own_start, block_rows)]
    own_half = w_kv_ref.at[pl.ds(pl.multiple_of(part * half_rows, half_rows), half_rows)]
    load_block = pltpu.make_async_copy(w_kv_ref, own_block, kl_sem)

    def kv_z(step):
        where = {"exp": 2 * peer(step) + side}
        return remote(
            own_half, block(z, side, part), zks_sem.at[step], zkr_sem.at[step], where
        )

    def kv_z_other(step):
        where = {"exp": 2 * peer(step) + side}
        piece = block(z, 1 - side, part)
        return remote(piece, piece, zls_sem.at[step], zlr_sem.at[step], where)

    def kv_x(step):
        piece = block(peer(step), side, part)
        source = own_half if step == 0 else piece
        return remote(source, piece, xks_sem.at[step], xkr_sem.at[step], {"exp": across})

    def kv_y(other, step):
        piece = block(peer(step), 1 - side if other else side, part)
        index = other * experts + step
        return remote(
            piece, piece, yks_sem.at[index], ykr_sem.at[index], {"rep": 1 - part}
        )

    def kv_core(late, other, step):
        index = (late * 2 + other) * experts + step
        where = {"dec": 1 - core}
        if other == 0 and step == 0:
            return remote(w_kv_ref, own_block, dks_sem.at[index], dkr_sem.at[index], where)
        half = 1 - part if late else part
        piece = block(peer(step), 1 - side if other else side, half)
        return remote(piece, piece, dks_sem.at[index], dkr_sem.at[index], where)

    pieces = [(0, step) for step in range(1, experts)] + [(1, step) for step in range(experts)]
    paired = [step for step in range(experts) if step % 2 == 0]
    unpaired = [step for step in range(experts) if step % 2 == 1]

    def got_own(step):
        kv_z(step).wait_recv()
        if step in paired:
            kv_x(step).start()
        kv_y(0, step).start()
        kv_core(0, 0, step).start()

    def got_other(step):
        if step in paired:
            kv_x(step).wait_recv()
        else:
            kv_z_other(step).wait_recv()
        if step == 0:
            for towards in unpaired:
                kv_z_other(towards).start()
        kv_y(1, step).start()
        kv_core(0, 1, step).start()

    def got_part(other, step):
        kv_y(other, step).wait_recv()
        kv_core(1, other, step).start()

    swap_weights = [
        remote(w_in_ref.at[0], wi.at[1], ws_sem.at[0], wr_sem.at[0], {"dec": 1 - core}),
        remote(w_out_ref.at[0], wo.at[1], ws_sem.at[1], wr_sem.at[1], {"dec": 1 - core}),
    ]

    def forward(step):
        at = peer(step)
        return remote(
            held.at[0, at], held.at[1, at], xs_sem.at[step], xr_sem.at[step], {"exp": across}
        )

    def part_copy(step):
        return remote(
            part_send.at[step],
            part_recv.at[step],
            ps_sem.at[step],
            pr_sem.at[step],
            {"exp": across},
        )

    def back_copy(step):
        return remote(
            back_send.at[step],
            back.at[z],
            bs_sem.at[step],
            br_sem.at[step],
            {"exp": 2 * peer(step) + side},
        )

    unit = wi.shape[2]
    tile = 512

    def ffn(column, at, store):
        def inner(i, carry):
            half = i // (unit // tile)
            offset = pl.multiple_of(i % (unit // tile) * tile, tile)
            block = jnp.dot(
                held[column, at],
                wi[half, :, pl.ds(offset, tile)],
                preferred_element_type=jnp.float32,
            )
            hid[half, :, pl.ds(offset, tile)] = jnp.maximum(block, 0.0).astype(jnp.bfloat16)
            return carry

        lax.fori_loop(0, 2 * (unit // tile), inner, 0)

        def outer(i, carry):
            cols = pl.ds(pl.multiple_of(i * tile, tile), tile)
            total = jnp.dot(hid[0], wo[0, :, cols], preferred_element_type=jnp.float32)
            total += jnp.dot(hid[1], wo[1, :, cols], preferred_element_type=jnp.float32)
            store(cols, total)
            return carry

        lax.fori_loop(0, width // tile, outer, 0)

    def ffn_own(step):
        def store(cols, total):
            own_sum[step, :, cols] = total

        ffn(0, peer(step), store)

    def ffn_other(step):
        def store(cols, total):
            part_send[step, :, cols] = total.astype(jnp.bfloat16)

        ffn(1, peer(step), store)
        part_copy(step).start()

    def finish(step):
        part_copy(step).wait_recv()
        total = (own_sum[step] + part_recv[step].astype(jnp.float32)).astype(jnp.bfloat16)
        if step == 0:
            back[z] = total
        else:
            back_send[step] = total
            back_copy(step).start()

    order = unpaired + paired[1:]
    for step in unpaired:
        dispatch(step).start()
    for step in unpaired:
        kv_z(step).start()
    for step in paired[1:]:
        dispatch(step).start()
    for step in paired[1:]:
        kv_z(step).start()
    held[0, z] = sends[z]
    forward(0).start()
    kv_x(0).start()
    for copy in swap_weights:
        copy.start()
    load_block.start()
    kv_core(0, 0, 0).start()
    for copy in local_weights:
        copy.wait()
    for copy in swap_weights:
        copy.wait_recv()
    ffn_own(0)
    for step in unpaired:
        dispatch(step).wait_recv()
        forward(step).start()
    got_other(0)
    for step in unpaired:
        got_own(step)
    previous = [0] + order[:-1]
    for at, step in enumerate(order):
        forward(previous[at]).wait_recv()
        ffn_other(previous[at])
        if at > 0:
            finish(previous[at - 1])
        if step in paired:
            dispatch(step).wait_recv()
            forward(step).start()
            got_own(step)
        ffn_own(step)
    for step in unpaired:
        got_other(step)
    forward(order[-1]).wait_recv()
    ffn_other(order[-1])
    for step in paired[1:]:
        got_other(step)
    got_part(1, 0)
    finish(previous[-1])
    for step in unpaired:
        got_part(0, step)
    finish(order[-1])
    for step in paired[1:]:
        got_part(0, step)
    for step in range(1, experts):
        got_part(1, step)

    logits = logits_t[...]
    gates = upright(jax.nn.sigmoid(logits[0:1] - logits[1:2]))
    gates_other = upright(jax.nn.sigmoid(logits[1:2] - logits[0:1]))
    residual = tok[...].astype(jnp.float32)
    for step in [0] + order:
        if step > 0:
            back_copy(step).wait_recv()
        e = peer(step)
        gate = jnp.where(first == e, gates, gates_other)
        residual += gate * jnp.dot(pick[e], back[e], preferred_element_type=jnp.float32)
    encoded = layer_norm(residual, final[...]).astype(jnp.bfloat16)
    mask = jnp.broadcast_to(live, (rows, 128)).astype(jnp.float32).astype(jnp.bfloat16)
    swap_send[:, :width] = encoded
    swap_send[:, width:] = mask
    exchange = remote(swap_send, swap_recv, es_sem, er_sem, {"dec": 1 - core})
    exchange.start()

    load_block.wait()
    kv_core(0, 0, 0).wait_recv()
    for other, step in pieces:
        kv_core(0, other, step).wait_recv()
        kv_core(1, other, step).wait_recv()
    exchange.wait_recv()
    keep = page_ref[0] == core
    kept = jnp.where(
        keep, swap_send[...].astype(jnp.float32), swap_recv[...].astype(jnp.float32)
    )
    rows_kept = kept[:, :width].astype(jnp.bfloat16)
    alive = kept[:, width : width + 1] > 0
    writes = []
    for i in range(kv.shape[1] // tile):
        cols = pl.ds(i * tile, tile)
        total = jnp.dot(rows_kept, wk[:, cols], preferred_element_type=jnp.float32)
        kv[:, cols] = jnp.where(alive, total + bias[:, cols], 0.0).astype(jnp.bfloat16)
        write = pltpu.make_async_copy(kv.at[:, cols], kv_ref.at[0, :, cols], kv_sem.at[i])
        write.start()
        writes.append(write)

    for copy in swap_weights:
        copy.wait_send()
    for step in range(experts):
        forward(step).wait_send()
        part_copy(step).wait_send()
        if step > 0:
            dispatch(step).wait_send()
            back_copy(step).wait_send()
            kv_z(step).wait_send()
        if step in paired:
            kv_x(step).wait_send()
        else:
            kv_z_other(step).wait_send()
    kv_core(0, 0, 0).wait_send()
    for other, step in pieces:
        kv_y(other, step).wait_send()
        kv_core(0, other, step).wait_send()
        kv_core(1, other, step).wait_send()
    exchange.wait_send()
    for write in writes:
        write.wait()


def kernel_shards(
    capacity,
    tokens,
    expert_ids,
    gate_logits,
    source_lengths,
    page_table,
    norm_gain,
    final_gain,
    w_in,
    w_out,
    w_kv,
    b_kv,
):
    rows, width = tokens.shape
    unit = w_in.shape[2]
    columns = w_kv.shape[1]
    experts = lax.axis_size("exp") // 2
    bf16 = jnp.bfloat16
    block = (experts, capacity, width)
    dma = pltpu.SemaphoreType.DMA
    scalar = pl.BlockSpec(memory_space=pltpu.SMEM)
    anywhere = pl.BlockSpec(memory_space=pl.ANY)
    return pl.pallas_call(
        functools.partial(fused_kernel, experts, capacity),
        out_shape=jax.ShapeDtypeStruct((1, rows, columns), bf16),
        in_specs=[anywhere] * 3 + [scalar] * 2 + [anywhere] * 6,
        out_specs=anywhere,
        scratch_shapes=[
            pltpu.VMEM((rows, width), bf16),
            pltpu.VMEM((2, rows), jnp.int32),
            pltpu.VMEM((2, rows), jnp.float32),
            pltpu.VMEM((1, width), jnp.float32),
            pltpu.VMEM((1, width), jnp.float32),
            pltpu.VMEM((1, columns), jnp.float32),
            pltpu.VMEM((rows, columns), bf16),
            pltpu.VMEM((width, columns), bf16),
            pltpu.VMEM((2,) + w_in.shape[1:], bf16),
            pltpu.VMEM((2,) + w_out.shape[1:], bf16),
            pltpu.VMEM((experts, rows, capacity), bf16),
            pltpu.VMEM(block, bf16),
            pltpu.VMEM((2,) + block, bf16),
            pltpu.VMEM((2, capacity, unit), bf16),
            pltpu.VMEM(block, jnp.float32),
            pltpu.VMEM(block, bf16),
            pltpu.VMEM(block, bf16),
            pltpu.VMEM(block, bf16),
            pltpu.VMEM(block, bf16),
            pltpu.VMEM((rows, width + 128), bf16),
            pltpu.VMEM((rows, width + 128), bf16),
            dma((2,)),
            dma((2,)),
            dma((2,)),
        ]
        + [dma((experts,)) for _ in range(8)]
        + [dma, dma, dma((6,)), dma]
        + [dma((experts,)) for _ in range(6)]
        + [dma((2 * experts,)) for _ in range(2)]
        + [dma((4 * experts,)) for _ in range(2)]
        + [dma((columns // 512,))],
        compiler_params=pltpu.CompilerParams(
            collective_id=0, has_side_effects=True, vmem_limit_bytes=60 * 1024 * 1024
        ),
        cost_estimate=pl.CostEstimate(
            flops=8 * experts * capacity * width * unit * 2,
            bytes_accessed=16 * 1024 * 1024,
            transcendentals=0,
        ),
        name="expert_layer",
    )(
        tokens,
        expert_ids.T,
        gate_logits.T,
        source_lengths,
        page_table,
        norm_gain.reshape(1, width),
        final_gain.reshape(1, width),
        w_in,
        w_out,
        w_kv,
        b_kv.reshape(1, columns),
    )


def any_shards(*args):
    tok_rows = args[0].shape[0]
    experts = lax.axis_size("exp") // 2
    capacity = 2 * max(1, (3 * tok_rows + experts - 1) // (2 * experts))
    whole_tiles = capacity % 16 == 0 and args[9].shape[0] % 32 == 0
    if whole_tiles and experts == 4 and lax.axis_size("dec") == lax.axis_size("rep") == 2:
        return kernel_shards(capacity, *args)
    return shards(*args)


def solution(mesh):
    return jax.shard_map(
        any_shards,
        mesh=mesh,
        in_specs=(
            P(("rep", "exp", "dec"), None),
            P(("rep", "exp", "dec"), None),
            P(("rep", "exp", "dec"), None),
            P(("rep", "exp", "dec")),
            P(("rep", "exp", "dec")),
            P(),
            P(),
            P("exp", None, "dec"),
            P("exp", "dec", None),
            P(("exp", "dec"), None),
            P(),
        ),
        out_specs=P(("rep", "exp", "dec"), None, None),
        check_vma=False,
    )
```

```python
import functools

import jax
import jax.numpy as jnp
from jax import lax
from jax.experimental import pallas as pl
from jax.experimental.pallas import tpu as pltpu
from jax.sharding import PartitionSpec as P

epsilon = 1e-05
MESH = pl.DeviceIdType.MESH


def partner(value, axis, bit):
    mask = 2**bit
    pairs = [(source, source ^ mask) for source in range(lax.axis_size(axis))]
    return lax.ppermute(value, axis, pairs)


def layer_norm(values, scale_gain):
    values = values.astype(jnp.float32)
    center = values - jnp.mean(values, axis=-1, keepdims=True)
    spread = jnp.mean(center * center, axis=-1, keepdims=True)
    return center * lax.rsqrt(spread + epsilon) * scale_gain


def route_slots(expert_ids, is_valid, experts):
    pair_ids = expert_ids.reshape(-1)
    pair_live = jnp.repeat(is_valid, 2)
    onehot = (
        (pair_ids[:, None] == jnp.arange(experts, dtype=jnp.int32)[None, :]) & pair_live[:, None]
    ).astype(jnp.int32)
    before = jnp.cumsum(onehot, axis=0) - onehot
    pair_slots = jnp.sum(before * onehot, axis=1)
    return (pair_ids, pair_live, pair_slots)


def shards(
    tokens,
    expert_ids,
    gate_logits,
    source_lengths,
    page_table,
    norm_gain,
    final_gain,
    w_in,
    w_out,
    w_kv,
    b_kv,
):
    tok_rows, feature_width = tokens.shape
    experts = lax.axis_size("exp") // 2
    capacity = 2 * max(1, (3 * tok_rows + experts - 1) // (2 * experts))
    half_cap = capacity // 2
    position = jnp.arange(tok_rows, dtype=jnp.int32)
    is_valid = position < source_lengths[0]
    normed = layer_norm(tokens, norm_gain).astype(jnp.bfloat16)
    pair_ids, pair_live, pair_slots = route_slots(expert_ids, is_valid, experts)
    overflow_row = experts * capacity
    target = jnp.where(pair_live, pair_ids * capacity + pair_slots, overflow_row)
    outgoing = (
        jnp.zeros((overflow_row, feature_width), jnp.bfloat16)
        .at[target]
        .set(jnp.repeat(normed, 2, axis=0), mode="drop")
    )
    arrived = lax.all_to_all(
        outgoing.reshape(2 * experts, half_cap, feature_width),
        "exp",
        split_axis=0,
        concat_axis=0,
        tiled=True,
    )
    partner_in, partner_out = partner((w_in, w_out), "exp", 0)
    w_inner = jnp.concatenate([w_in[0], partner_in[0]], axis=1)
    w_outer = jnp.concatenate([w_out[0], partner_out[0]], axis=0)
    local_rows = arrived[None]
    block_piece = lax.all_gather(local_rows[None], "dec", axis=0, tiled=True)
    flat_rows = block_piece.reshape(-1, feature_width)
    hidden = jnp.maximum(
        jnp.dot(flat_rows, w_inner, preferred_element_type=jnp.float32), 0.0
    ).astype(jnp.bfloat16)
    partial_out = jnp.dot(hidden, w_outer, preferred_element_type=jnp.float32).reshape(
        block_piece.shape
    )
    summed = partial_out[:, 0]
    reduced = lax.psum_scatter(summed, "dec", scatter_dimension=0, tiled=True)[0].astype(
        jnp.bfloat16
    )
    returned = lax.all_to_all(reduced, "exp", split_axis=0, concat_axis=0, tiled=True).reshape(
        overflow_row, feature_width
    )
    picked = (
        returned[jnp.minimum(target, overflow_row - 1)]
        .astype(jnp.float32)
        .reshape(tok_rows, 2, feature_width)
    )
    gate_weights = jax.nn.sigmoid(gate_logits - gate_logits[:, ::-1])
    mixed_out = jnp.sum(gate_weights[:, :, None] * picked, axis=1)
    residual_sum = tokens.astype(jnp.float32) + jnp.where(is_valid[:, None], mixed_out, 0.0)
    encoded = layer_norm(residual_sum, final_gain).astype(jnp.bfloat16)
    my_core = lax.axis_index("dec")
    keep_own = page_table[0] == my_core
    page_length = source_lengths[0]
    projected = jnp.dot(
        encoded,
        lax.all_gather(w_kv, ("exp", "dec"), axis=0, tiled=True),
        preferred_element_type=jnp.float32,
    )
    keys_values = jnp.where((position < page_length)[:, None], projected + b_kv, 0.0).astype(
        jnp.bfloat16
    )
    page_result = jnp.where(keep_own, keys_values, partner(keys_values, "dec", 0))
    return page_result[None]


def fused_kernel(
    experts,
    capacity,
    tokens_ref,
    ids_ref,
    logits_ref,
    length_ref,
    page_ref,
    norm_ref,
    final_ref,
    w_in_ref,
    w_out_ref,
    w_kv_ref,
    b_kv_ref,
    kv_ref,
    tok,
    ids_t,
    logits_t,
    norm,
    final,
    bias,
    kv,
    wk,
    wi,
    wo,
    pick,
    sends,
    held,
    hid,
    own_sum,
    part_send,
    part_recv,
    back_send,
    back,
    swap_send,
    swap_recv,
    wl_sem,
    ws_sem,
    wr_sem,
    zs_sem,
    zr_sem,
    xs_sem,
    xr_sem,
    ps_sem,
    pr_sem,
    bs_sem,
    br_sem,
    es_sem,
    er_sem,
    in_sem,
    kl_sem,
    zks_sem,
    zkr_sem,
    zls_sem,
    zlr_sem,
    xks_sem,
    xkr_sem,
    yks_sem,
    ykr_sem,
    dks_sem,
    dkr_sem,
    kv_sem,
):
    rows, width = tokens_ref.shape
    group = lax.axis_index("exp")
    part = lax.axis_index("rep")
    core = lax.axis_index("dec")
    z = group // 2
    side = group % 2
    across = 2 * z + (1 - side)

    def peer(step):
        other, bit = 0, 1
        while bit < experts:
            mine, flip = (z // bit) % 2, (step // bit) % 2
            other = other + bit * (mine + flip - 2 * mine * flip)
            bit *= 2
        return other

    inputs = [
        pltpu.make_async_copy(src, dst, in_sem.at[i])
        for i, (src, dst) in enumerate(
            (
                (tokens_ref, tok),
                (ids_ref, ids_t),
                (logits_ref, logits_t),
                (norm_ref, norm),
                (final_ref, final),
                (b_kv_ref, bias),
            )
        )
    ]
    for copy in inputs:
        copy.start()

    barrier = pltpu.get_barrier_semaphore()
    pl.semaphore_signal(barrier, inc=1, device_id={"dec": 1 - core}, device_id_type=MESH)
    pl.semaphore_signal(barrier, inc=1, device_id={"exp": across}, device_id_type=MESH)
    pl.semaphore_signal(barrier, inc=1, device_id={"rep": 1 - part}, device_id_type=MESH)
    for step in range(1, experts):
        pl.semaphore_signal(
            barrier, inc=1, device_id={"exp": 2 * peer(step) + side}, device_id_type=MESH
        )

    local_weights = [
        pltpu.make_async_copy(w_in_ref.at[0], wi.at[0], wl_sem.at[0]),
        pltpu.make_async_copy(w_out_ref.at[0], wo.at[0], wl_sem.at[1]),
    ]
    for copy in local_weights:
        copy.start()

    for copy in inputs:
        copy.wait()
    normed = layer_norm(tok[...], norm[...]).astype(jnp.bfloat16)
    row = lax.broadcasted_iota(jnp.int32, (rows, rows), 0)
    column = lax.broadcasted_iota(jnp.int32, (rows, rows), 1)

    def upright(line):
        return jnp.sum(jnp.where(row == column, line, 0.0), axis=1, keepdims=True)

    ids_f = ids_t[...].astype(jnp.float32)
    first, second = (upright(ids_f[k : k + 1]).astype(jnp.int32) for k in range(2))
    live = lax.broadcasted_iota(jnp.int32, (rows, 1), 0) < length_ref[0]
    lane = lax.broadcasted_iota(jnp.int32, (rows, 128), 1)
    named = ((first == lane) | (second == lane)) & live
    earlier = column < row
    count = jnp.dot(
        earlier.astype(jnp.float32).astype(jnp.bfloat16),
        named.astype(jnp.float32).astype(jnp.bfloat16),
        preferred_element_type=jnp.float32,
    ).astype(jnp.int32)
    slots = jnp.where(named, count, -1)
    slot_lane = lax.broadcasted_iota(jnp.int32, (rows, capacity), 1)
    for e in range(experts):
        chosen = (slots[:, e : e + 1] == slot_lane).astype(jnp.float32).astype(jnp.bfloat16)
        pick[e] = chosen
        sends[e] = lax.dot_general(
            chosen, normed, (((0,), (0,)), ((), ())), preferred_element_type=jnp.float32
        ).astype(jnp.bfloat16)

    pl.semaphore_wait(barrier, experts + 2)

    def remote(src, dst, send_sem, recv_sem, where):
        return pltpu.make_async_remote_copy(
            src_ref=src,
            dst_ref=dst,
            send_sem=send_sem,
            recv_sem=recv_sem,
            device_id=where,
            device_id_type=MESH,
        )

    def dispatch(step):
        to = peer(step)
        return remote(
            sends.at[to],
            held.at[0, z],
            zs_sem.at[step],
            zr_sem.at[step],
            {"exp": 2 * to + side},
        )

    block_rows = w_kv_ref.shape[0]
    half_rows = block_rows // 2

    def block(at, column_side, half):
        start = ((2 * at + column_side) * 2 + core) * block_rows + half * half_rows
        return wk.at[pl.ds(pl.multiple_of(start, half_rows), half_rows)]

    own_start = pl.multiple_of((2 * group + core) * block_rows, block_rows)
    own_block = wk.at[pl.ds(own_start, block_rows)]
    own_half = w_kv_ref.at[pl.ds(pl.multiple_of(part * half_rows, half_rows), half_rows)]
    load_block = pltpu.make_async_copy(w_kv_ref, own_block, kl_sem)

    def kv_z(step):
        where = {"exp": 2 * peer(step) + side}
        return remote(
            own_half, block(z, side, part), zks_sem.at[step], zkr_sem.at[step], where
        )

    def kv_z_other(step):
        where = {"exp": 2 * peer(step) + side}
        piece = block(z, 1 - side, part)
        return remote(piece, piece, zls_sem.at[step], zlr_sem.at[step], where)

    def kv_x(step):
        piece = block(peer(step), side, part)
        source = own_half if step == 0 else piece
        return remote(source, piece, xks_sem.at[step], xkr_sem.at[step], {"exp": across})

    def kv_y(other, step):
        piece = block(peer(step), 1 - side if other else side, part)
        index = other * experts + step
        return remote(
            piece, piece, yks_sem.at[index], ykr_sem.at[index], {"rep": 1 - part}
        )

    def kv_core(late, other, step):
        index = (late * 2 + other) * experts + step
        where = {"dec": 1 - core}
        if other == 0 and step == 0:
            return remote(w_kv_ref, own_block, dks_sem.at[index], dkr_sem.at[index], where)
        half = 1 - part if late else part
        piece = block(peer(step), 1 - side if other else side, half)
        return remote(piece, piece, dks_sem.at[index], dkr_sem.at[index], where)

    pieces = [(0, step) for step in range(1, experts)] + [(1, step) for step in range(experts)]
    paired = [step for step in range(experts) if step % 2 == 0]
    unpaired = [step for step in range(experts) if step % 2 == 1]

    def got_own(step):
        kv_z(step).wait_recv()
        if step in paired:
            kv_x(step).start()
        kv_y(0, step).start()
        kv_core(0, 0, step).start()

    def got_other(step):
        if step in paired:
            kv_x(step).wait_recv()
        else:
            kv_z_other(step).wait_recv()
        if step == 0:
            for towards in unpaired:
                kv_z_other(towards).start()
        kv_y(1, step).start()
        kv_core(0, 1, step).start()

    def got_part(other, step):
        kv_y(other, step).wait_recv()
        kv_core(1, other, step).start()

    swap_weights = [
        remote(w_in_ref.at[0], wi.at[1], ws_sem.at[0], wr_sem.at[0], {"dec": 1 - core}),
        remote(w_out_ref.at[0], wo.at[1], ws_sem.at[1], wr_sem.at[1], {"dec": 1 - core}),
    ]

    def forward(step):
        at = peer(step)
        return remote(
            held.at[0, at], held.at[1, at], xs_sem.at[step], xr_sem.at[step], {"exp": across}
        )

    def part_copy(step):
        return remote(
            part_send.at[step],
            part_recv.at[step],
            ps_sem.at[step],
            pr_sem.at[step],
            {"exp": across},
        )

    def back_copy(step):
        return remote(
            back_send.at[step],
            back.at[z],
            bs_sem.at[step],
            br_sem.at[step],
            {"exp": 2 * peer(step) + side},
        )

    unit = wi.shape[2]
    tile = 512

    def ffn(column, at, store):
        def inner(i, carry):
            half = i // (unit // tile)
            offset = pl.multiple_of(i % (unit // tile) * tile, tile)
            block = jnp.dot(
                held[column, at],
                wi[half, :, pl.ds(offset, tile)],
                preferred_element_type=jnp.float32,
            )
            hid[half, :, pl.ds(offset, tile)] = jnp.maximum(block, 0.0).astype(jnp.bfloat16)
            return carry

        lax.fori_loop(0, 2 * (unit // tile), inner, 0)

        def outer(i, carry):
            cols = pl.ds(pl.multiple_of(i * tile, tile), tile)
            total = jnp.dot(hid[0], wo[0, :, cols], preferred_element_type=jnp.float32)
            total += jnp.dot(hid[1], wo[1, :, cols], preferred_element_type=jnp.float32)
            store(cols, total)
            return carry

        lax.fori_loop(0, width // tile, outer, 0)

    def ffn_own(step):
        def store(cols, total):
            own_sum[step, :, cols] = total

        ffn(0, peer(step), store)

    def ffn_other(step):
        def store(cols, total):
            part_send[step, :, cols] = total.astype(jnp.bfloat16)

        ffn(1, peer(step), store)
        part_copy(step).start()

    def finish(step):
        part_copy(step).wait_recv()
        total = (own_sum[step] + part_recv[step].astype(jnp.float32)).astype(jnp.bfloat16)
        if step == 0:
            back[z] = total
        else:
            back_send[step] = total
            back_copy(step).start()

    for step in unpaired:
        dispatch(step).start()
    for step in unpaired:
        kv_z(step).start()
    for step in paired[1:]:
        dispatch(step).start()
    for step in paired[1:]:
        kv_z(step).start()
    held[0, z] = sends[z]
    forward(0).start()
    kv_x(0).start()
    for copy in swap_weights:
        copy.start()
    load_block.start()
    kv_core(0, 0, 0).start()
    for copy in local_weights:
        copy.wait()
    for copy in swap_weights:
        copy.wait_recv()
    ffn_own(0)
    near, far = unpaired, paired[1:]
    for step in near:
        dispatch(step).wait_recv()
        forward(step).start()
    got_other(0)
    for step in near:
        got_own(step)
    for step in near:
        ffn_own(step)
        forward(step).wait_recv()
        ffn_other(step)
        if step == near[0]:
            for distant in far:
                dispatch(distant).wait_recv()
                forward(distant).start()
                got_own(distant)
    for step in far:
        ffn_own(step)
    for step in near:
        got_other(step)
    for step in far:
        forward(step).wait_recv()
        ffn_other(step)
    forward(0).wait_recv()
    ffn_other(0)
    finish(near[0])
    got_part(1, 0)
    for step in near[1:]:
        finish(step)
    for step in near:
        got_part(0, step)
    for step in far:
        got_other(step)
        finish(step)
    for step in near:
        got_part(1, step)
    for step in far:
        got_part(0, step)
    finish(0)
    for step in far:
        got_part(1, step)

    logits = logits_t[...]
    gates = upright(jax.nn.sigmoid(logits[0:1] - logits[1:2]))
    gates_other = upright(jax.nn.sigmoid(logits[1:2] - logits[0:1]))
    residual = tok[...].astype(jnp.float32)
    for step in near + [0] + far:
        if step > 0:
            back_copy(step).wait_recv()
        e = peer(step)
        gate = jnp.where(first == e, gates, gates_other)
        residual += gate * jnp.dot(pick[e], back[e], preferred_element_type=jnp.float32)
    encoded = layer_norm(residual, final[...]).astype(jnp.bfloat16)
    mask = jnp.broadcast_to(live, (rows, 128)).astype(jnp.float32).astype(jnp.bfloat16)
    swap_send[:, :width] = encoded
    swap_send[:, width:] = mask
    exchange = remote(swap_send, swap_recv, es_sem, er_sem, {"dec": 1 - core})
    exchange.start()

    load_block.wait()
    kv_core(0, 0, 0).wait_recv()
    for other, step in pieces:
        kv_core(0, other, step).wait_recv()
        kv_core(1, other, step).wait_recv()
    exchange.wait_recv()
    keep = page_ref[0] == core
    kept = jnp.where(
        keep, swap_send[...].astype(jnp.float32), swap_recv[...].astype(jnp.float32)
    )
    rows_kept = kept[:, :width].astype(jnp.bfloat16)
    alive = kept[:, width : width + 1] > 0
    writes = []
    for i in range(kv.shape[1] // tile):
        cols = pl.ds(i * tile, tile)
        total = jnp.dot(rows_kept, wk[:, cols], preferred_element_type=jnp.float32)
        kv[:, cols] = jnp.where(alive, total + bias[:, cols], 0.0).astype(jnp.bfloat16)
        write = pltpu.make_async_copy(kv.at[:, cols], kv_ref.at[0, :, cols], kv_sem.at[i])
        write.start()
        writes.append(write)

    for copy in swap_weights:
        copy.wait_send()
    for step in range(experts):
        forward(step).wait_send()
        part_copy(step).wait_send()
        if step > 0:
            dispatch(step).wait_send()
            back_copy(step).wait_send()
            kv_z(step).wait_send()
        if step in paired:
            kv_x(step).wait_send()
        else:
            kv_z_other(step).wait_send()
    kv_core(0, 0, 0).wait_send()
    for other, step in pieces:
        kv_y(other, step).wait_send()
        kv_core(0, other, step).wait_send()
        kv_core(1, other, step).wait_send()
    exchange.wait_send()
    for write in writes:
        write.wait()


def kernel_shards(
    capacity,
    tokens,
    expert_ids,
    gate_logits,
    source_lengths,
    page_table,
    norm_gain,
    final_gain,
    w_in,
    w_out,
    w_kv,
    b_kv,
):
    rows, width = tokens.shape
    unit = w_in.shape[2]
    columns = w_kv.shape[1]
    experts = lax.axis_size("exp") // 2
    bf16 = jnp.bfloat16
    block = (experts, capacity, width)
    dma = pltpu.SemaphoreType.DMA
    scalar = pl.BlockSpec(memory_space=pltpu.SMEM)
    anywhere = pl.BlockSpec(memory_space=pl.ANY)
    return pl.pallas_call(
        functools.partial(fused_kernel, experts, capacity),
        out_shape=jax.ShapeDtypeStruct((1, rows, columns), bf16),
        in_specs=[anywhere] * 3 + [scalar] * 2 + [anywhere] * 6,
        out_specs=anywhere,
        scratch_shapes=[
            pltpu.VMEM((rows, width), bf16),
            pltpu.VMEM((2, rows), jnp.int32),
            pltpu.VMEM((2, rows), jnp.float32),
            pltpu.VMEM((1, width), jnp.float32),
            pltpu.VMEM((1, width), jnp.float32),
            pltpu.VMEM((1, columns), jnp.float32),
            pltpu.VMEM((rows, columns), bf16),
            pltpu.VMEM((width, columns), bf16),
            pltpu.VMEM((2,) + w_in.shape[1:], bf16),
            pltpu.VMEM((2,) + w_out.shape[1:], bf16),
            pltpu.VMEM((experts, rows, capacity), bf16),
            pltpu.VMEM(block, bf16),
            pltpu.VMEM((2,) + block, bf16),
            pltpu.VMEM((2, capacity, unit), bf16),
            pltpu.VMEM(block, jnp.float32),
            pltpu.VMEM(block, bf16),
            pltpu.VMEM(block, bf16),
            pltpu.VMEM(block, bf16),
            pltpu.VMEM(block, bf16),
            pltpu.VMEM((rows, width + 128), bf16),
            pltpu.VMEM((rows, width + 128), bf16),
            dma((2,)),
            dma((2,)),
            dma((2,)),
        ]
        + [dma((experts,)) for _ in range(8)]
        + [dma, dma, dma((6,)), dma]
        + [dma((experts,)) for _ in range(6)]
        + [dma((2 * experts,)) for _ in range(2)]
        + [dma((4 * experts,)) for _ in range(2)]
        + [dma((columns // 512,))],
        compiler_params=pltpu.CompilerParams(
            collective_id=0, has_side_effects=True, vmem_limit_bytes=60 * 1024 * 1024
        ),
        cost_estimate=pl.CostEstimate(
            flops=8 * experts * capacity * width * unit * 2,
            bytes_accessed=16 * 1024 * 1024,
            transcendentals=0,
        ),
        name="expert_layer",
    )(
        tokens,
        expert_ids.T,
        gate_logits.T,
        source_lengths,
        page_table,
        norm_gain.reshape(1, width),
        final_gain.reshape(1, width),
        w_in,
        w_out,
        w_kv,
        b_kv.reshape(1, columns),
    )


def any_shards(*args):
    tok_rows = args[0].shape[0]
    experts = lax.axis_size("exp") // 2
    capacity = 2 * max(1, (3 * tok_rows + experts - 1) // (2 * experts))
    whole_tiles = capacity % 16 == 0 and args[9].shape[0] % 32 == 0
    if whole_tiles and experts == 4 and lax.axis_size("dec") == lax.axis_size("rep") == 2:
        return kernel_shards(capacity, *args)
    return shards(*args)


def solution(mesh):
    return jax.shard_map(
        any_shards,
        mesh=mesh,
        in_specs=(
            P(("rep", "exp", "dec"), None),
            P(("rep", "exp", "dec"), None),
            P(("rep", "exp", "dec"), None),
            P(("rep", "exp", "dec")),
            P(("rep", "exp", "dec")),
            P(),
            P(),
            P("exp", None, "dec"),
            P("exp", "dec", None),
            P(("exp", "dec"), None),
            P(),
        ),
        out_specs=P(("rep", "exp", "dec"), None, None),
        check_vma=False,
    )
```

```python
import functools

import jax
import jax.numpy as jnp
from jax import lax
from jax.experimental import pallas as pl
from jax.experimental.pallas import tpu as pltpu
from jax.sharding import PartitionSpec as P

epsilon = 1e-05
MESH = pl.DeviceIdType.MESH


def partner(value, axis, bit):
    mask = 2**bit
    pairs = [(source, source ^ mask) for source in range(lax.axis_size(axis))]
    return lax.ppermute(value, axis, pairs)


def layer_norm(values, scale_gain):
    values = values.astype(jnp.float32)
    center = values - jnp.mean(values, axis=-1, keepdims=True)
    spread = jnp.mean(center * center, axis=-1, keepdims=True)
    return center * lax.rsqrt(spread + epsilon) * scale_gain


def route_slots(expert_ids, is_valid, experts):
    pair_ids = expert_ids.reshape(-1)
    pair_live = jnp.repeat(is_valid, 2)
    onehot = (
        (pair_ids[:, None] == jnp.arange(experts, dtype=jnp.int32)[None, :]) & pair_live[:, None]
    ).astype(jnp.int32)
    before = jnp.cumsum(onehot, axis=0) - onehot
    pair_slots = jnp.sum(before * onehot, axis=1)
    return (pair_ids, pair_live, pair_slots)


def shards(
    tokens,
    expert_ids,
    gate_logits,
    source_lengths,
    page_table,
    norm_gain,
    final_gain,
    w_in,
    w_out,
    w_kv,
    b_kv,
):
    tok_rows, feature_width = tokens.shape
    experts = lax.axis_size("exp") // 2
    capacity = 2 * max(1, (3 * tok_rows + experts - 1) // (2 * experts))
    half_cap = capacity // 2
    position = jnp.arange(tok_rows, dtype=jnp.int32)
    is_valid = position < source_lengths[0]
    normed = layer_norm(tokens, norm_gain).astype(jnp.bfloat16)
    pair_ids, pair_live, pair_slots = route_slots(expert_ids, is_valid, experts)
    overflow_row = experts * capacity
    target = jnp.where(pair_live, pair_ids * capacity + pair_slots, overflow_row)
    outgoing = (
        jnp.zeros((overflow_row, feature_width), jnp.bfloat16)
        .at[target]
        .set(jnp.repeat(normed, 2, axis=0), mode="drop")
    )
    arrived = lax.all_to_all(
        outgoing.reshape(2 * experts, half_cap, feature_width),
        "exp",
        split_axis=0,
        concat_axis=0,
        tiled=True,
    )
    partner_in, partner_out = partner((w_in, w_out), "exp", 0)
    w_inner = jnp.concatenate([w_in[0], partner_in[0]], axis=1)
    w_outer = jnp.concatenate([w_out[0], partner_out[0]], axis=0)
    local_rows = arrived[None]
    block_piece = lax.all_gather(local_rows[None], "dec", axis=0, tiled=True)
    flat_rows = block_piece.reshape(-1, feature_width)
    hidden = jnp.maximum(
        jnp.dot(flat_rows, w_inner, preferred_element_type=jnp.float32), 0.0
    ).astype(jnp.bfloat16)
    partial_out = jnp.dot(hidden, w_outer, preferred_element_type=jnp.float32).reshape(
        block_piece.shape
    )
    summed = partial_out[:, 0]
    reduced = lax.psum_scatter(summed, "dec", scatter_dimension=0, tiled=True)[0].astype(
        jnp.bfloat16
    )
    returned = lax.all_to_all(reduced, "exp", split_axis=0, concat_axis=0, tiled=True).reshape(
        overflow_row, feature_width
    )
    picked = (
        returned[jnp.minimum(target, overflow_row - 1)]
        .astype(jnp.float32)
        .reshape(tok_rows, 2, feature_width)
    )
    gate_weights = jax.nn.sigmoid(gate_logits - gate_logits[:, ::-1])
    mixed_out = jnp.sum(gate_weights[:, :, None] * picked, axis=1)
    residual_sum = tokens.astype(jnp.float32) + jnp.where(is_valid[:, None], mixed_out, 0.0)
    encoded = layer_norm(residual_sum, final_gain).astype(jnp.bfloat16)
    my_core = lax.axis_index("dec")
    keep_own = page_table[0] == my_core
    page_length = source_lengths[0]
    projected = jnp.dot(
        encoded,
        lax.all_gather(w_kv, ("exp", "dec"), axis=0, tiled=True),
        preferred_element_type=jnp.float32,
    )
    keys_values = jnp.where((position < page_length)[:, None], projected + b_kv, 0.0).astype(
        jnp.bfloat16
    )
    page_result = jnp.where(keep_own, keys_values, partner(keys_values, "dec", 0))
    return page_result[None]


def fused_kernel(
    experts,
    capacity,
    tokens_ref,
    ids_ref,
    logits_ref,
    length_ref,
    page_ref,
    norm_ref,
    final_ref,
    w_in_ref,
    w_out_ref,
    w_kv_ref,
    b_kv_ref,
    kv_ref,
    tok,
    ids_t,
    logits_t,
    norm,
    final,
    bias,
    kv,
    wk,
    wi,
    wo,
    pick,
    sends,
    held,
    hid,
    own_sum,
    part_send,
    part_recv,
    back_send,
    back,
    swap_send,
    swap_recv,
    wl_sem,
    ws_sem,
    wr_sem,
    zs_sem,
    zr_sem,
    xs_sem,
    xr_sem,
    ps_sem,
    pr_sem,
    bs_sem,
    br_sem,
    es_sem,
    er_sem,
    in_sem,
    kl_sem,
    zks_sem,
    zkr_sem,
    zls_sem,
    zlr_sem,
    xks_sem,
    xkr_sem,
    yks_sem,
    ykr_sem,
    dks_sem,
    dkr_sem,
    kv_sem,
):
    rows, width = tokens_ref.shape
    group = lax.axis_index("exp")
    part = lax.axis_index("rep")
    core = lax.axis_index("dec")
    z = group // 2
    side = group % 2
    across = 2 * z + (1 - side)

    def peer(step):
        other, bit = 0, 1
        while bit < experts:
            mine, flip = (z // bit) % 2, (step // bit) % 2
            other = other + bit * (mine + flip - 2 * mine * flip)
            bit *= 2
        return other

    inputs = [
        pltpu.make_async_copy(src, dst, in_sem.at[i])
        for i, (src, dst) in enumerate(
            (
                (tokens_ref, tok),
                (ids_ref, ids_t),
                (logits_ref, logits_t),
                (norm_ref, norm),
                (final_ref, final),
                (b_kv_ref, bias),
            )
        )
    ]
    for copy in inputs:
        copy.start()

    barrier = pltpu.get_barrier_semaphore()
    pl.semaphore_signal(barrier, inc=1, device_id={"dec": 1 - core}, device_id_type=MESH)
    pl.semaphore_signal(barrier, inc=1, device_id={"exp": across}, device_id_type=MESH)
    pl.semaphore_signal(barrier, inc=1, device_id={"rep": 1 - part}, device_id_type=MESH)
    for step in range(1, experts):
        pl.semaphore_signal(
            barrier, inc=1, device_id={"exp": 2 * peer(step) + side}, device_id_type=MESH
        )

    local_weights = [
        pltpu.make_async_copy(w_in_ref.at[0], wi.at[0], wl_sem.at[0]),
        pltpu.make_async_copy(w_out_ref.at[0], wo.at[0], wl_sem.at[1]),
    ]
    for copy in local_weights:
        copy.start()

    for copy in inputs:
        copy.wait()
    normed = layer_norm(tok[...], norm[...]).astype(jnp.bfloat16)
    row = lax.broadcasted_iota(jnp.int32, (rows, rows), 0)
    column = lax.broadcasted_iota(jnp.int32, (rows, rows), 1)

    def upright(line):
        return jnp.sum(jnp.where(row == column, line, 0.0), axis=1, keepdims=True)

    ids_f = ids_t[...].astype(jnp.float32)
    first, second = (upright(ids_f[k : k + 1]).astype(jnp.int32) for k in range(2))
    live = lax.broadcasted_iota(jnp.int32, (rows, 1), 0) < length_ref[0]
    lane = lax.broadcasted_iota(jnp.int32, (rows, 128), 1)
    named = ((first == lane) | (second == lane)) & live
    earlier = column < row
    count = jnp.dot(
        earlier.astype(jnp.float32).astype(jnp.bfloat16),
        named.astype(jnp.float32).astype(jnp.bfloat16),
        preferred_element_type=jnp.float32,
    ).astype(jnp.int32)
    slots = jnp.where(named, count, -1)
    slot_lane = lax.broadcasted_iota(jnp.int32, (rows, capacity), 1)
    pl.semaphore_wait(barrier, experts + 2)

    def remote(src, dst, send_sem, recv_sem, where):
        return pltpu.make_async_remote_copy(
            src_ref=src,
            dst_ref=dst,
            send_sem=send_sem,
            recv_sem=recv_sem,
            device_id=where,
            device_id_type=MESH,
        )

    def dispatch(step):
        to = peer(step)
        return remote(
            sends.at[to],
            held.at[0, z],
            zs_sem.at[step],
            zr_sem.at[step],
            {"exp": 2 * to + side},
        )

    block_rows = w_kv_ref.shape[0]
    half_rows = block_rows // 2

    def block(at, column_side, half):
        start = ((2 * at + column_side) * 2 + core) * block_rows + half * half_rows
        return wk.at[pl.ds(pl.multiple_of(start, half_rows), half_rows)]

    own_start = pl.multiple_of((2 * group + core) * block_rows, block_rows)
    own_block = wk.at[pl.ds(own_start, block_rows)]
    own_half = w_kv_ref.at[pl.ds(pl.multiple_of(part * half_rows, half_rows), half_rows)]
    load_block = pltpu.make_async_copy(w_kv_ref, own_block, kl_sem)

    def kv_z(step):
        where = {"exp": 2 * peer(step) + side}
        return remote(
            own_half, block(z, side, part), zks_sem.at[step], zkr_sem.at[step], where
        )

    def kv_z_other(step):
        where = {"exp": 2 * peer(step) + side}
        piece = block(z, 1 - side, part)
        return remote(piece, piece, zls_sem.at[step], zlr_sem.at[step], where)

    def kv_x(step):
        piece = block(peer(step), side, part)
        source = own_half if step == 0 else piece
        return remote(source, piece, xks_sem.at[step], xkr_sem.at[step], {"exp": across})

    def kv_y(other, step):
        piece = block(peer(step), 1 - side if other else side, part)
        index = other * experts + step
        return remote(
            piece, piece, yks_sem.at[index], ykr_sem.at[index], {"rep": 1 - part}
        )

    def kv_core(late, other, step):
        index = (late * 2 + other) * experts + step
        where = {"dec": 1 - core}
        if other == 0 and step == 0:
            return remote(w_kv_ref, own_block, dks_sem.at[index], dkr_sem.at[index], where)
        half = 1 - part if late else part
        piece = block(peer(step), 1 - side if other else side, half)
        return remote(piece, piece, dks_sem.at[index], dkr_sem.at[index], where)

    pieces = [(0, step) for step in range(1, experts)] + [(1, step) for step in range(experts)]
    paired = [step for step in range(experts) if step % 2 == 0]
    unpaired = [step for step in range(experts) if step % 2 == 1]

    def got_own(step):
        kv_z(step).wait_recv()
        if step in paired:
            kv_x(step).start()
        kv_y(0, step).start()
        kv_core(0, 0, step).start()

    def got_other(step):
        if step in paired:
            kv_x(step).wait_recv()
        else:
            kv_z_other(step).wait_recv()
        if step == 0:
            for towards in unpaired:
                kv_z_other(towards).start()
        kv_y(1, step).start()
        kv_core(0, 1, step).start()

    def got_part(other, step):
        kv_y(other, step).wait_recv()
        kv_core(1, other, step).start()

    swap_weights = [
        remote(w_in_ref.at[0], wi.at[1], ws_sem.at[0], wr_sem.at[0], {"dec": 1 - core}),
        remote(w_out_ref.at[0], wo.at[1], ws_sem.at[1], wr_sem.at[1], {"dec": 1 - core}),
    ]

    def forward(step):
        at = peer(step)
        return remote(
            held.at[0, at], held.at[1, at], xs_sem.at[step], xr_sem.at[step], {"exp": across}
        )

    def part_copy(step):
        return remote(
            part_send.at[step],
            part_recv.at[step],
            ps_sem.at[step],
            pr_sem.at[step],
            {"exp": across},
        )

    def back_copy(step):
        return remote(
            back_send.at[step],
            back.at[z],
            bs_sem.at[step],
            br_sem.at[step],
            {"exp": 2 * peer(step) + side},
        )

    unit = wi.shape[2]
    tile = 512

    def ffn(column, at, store):
        def inner(i, carry):
            half = i // (unit // tile)
            offset = pl.multiple_of(i % (unit // tile) * tile, tile)
            block = jnp.dot(
                held[column, at],
                wi[half, :, pl.ds(offset, tile)],
                preferred_element_type=jnp.float32,
            )
            hid[half, :, pl.ds(offset, tile)] = jnp.maximum(block, 0.0).astype(jnp.bfloat16)
            return carry

        lax.fori_loop(0, 2 * (unit // tile), inner, 0)

        def outer(i, carry):
            cols = pl.ds(pl.multiple_of(i * tile, tile), tile)
            total = jnp.dot(hid[0], wo[0, :, cols], preferred_element_type=jnp.float32)
            total += jnp.dot(hid[1], wo[1, :, cols], preferred_element_type=jnp.float32)
            store(cols, total)
            return carry

        lax.fori_loop(0, width // tile, outer, 0)

    def ffn_own(step):
        def store(cols, total):
            own_sum[step, :, cols] = total

        ffn(0, peer(step), store)

    def ffn_other(step):
        def store(cols, total):
            part_send[step, :, cols] = total.astype(jnp.bfloat16)

        ffn(1, peer(step), store)
        part_copy(step).start()

    def finish(step):
        part_copy(step).wait_recv()
        total = (own_sum[step] + part_recv[step].astype(jnp.float32)).astype(jnp.bfloat16)
        if step == 0:
            back[z] = total
        else:
            back_send[step] = total
            back_copy(step).start()

    for copy in swap_weights:
        copy.start()
    near, far = unpaired, paired[1:]
    for step in near + [0] + far:
        e = peer(step)
        slot = jnp.sum(jnp.where(lane == e, slots, 0), axis=1, keepdims=True)
        chosen = (slot == slot_lane).astype(jnp.float32).astype(jnp.bfloat16)
        pick[e] = chosen
        gathered = lax.dot_general(
            chosen, normed, (((0,), (0,)), ((), ())), preferred_element_type=jnp.float32
        ).astype(jnp.bfloat16)
        if step == 0:
            held[0, z] = gathered
            forward(0).start()
        else:
            sends[e] = gathered
            dispatch(step).start()
    kv_x(0).start()
    for step in near + far:
        kv_z(step).start()
    load_block.start()
    kv_core(0, 0, 0).start()
    for copy in local_weights:
        copy.wait()
    for copy in swap_weights:
        copy.wait_recv()
    ffn_own(0)
    for step in near:
        dispatch(step).wait_recv()
        forward(step).start()
        if step == near[0]:
            forward(0).wait_recv()
            ffn_other(0)
    got_other(0)
    got_own(near[0])
    ffn_own(near[0])
    for step in far:
        dispatch(step).wait_recv()
        forward(step).start()
    forward(near[0]).wait_recv()
    ffn_other(near[0])
    for step in near[1:] + far:
        got_own(step)
        ffn_own(step)
    finish(0)
    for step in far + near[1:]:
        forward(step).wait_recv()
        ffn_other(step)
    got_part(1, 0)
    for step in near:
        got_other(step)
    finish(near[0])
    for step in near:
        got_part(0, step)
    for step in far:
        got_other(step)
    for step in far + near[1:]:
        finish(step)
    for step in near:
        got_part(1, step)
    for step in far:
        got_part(0, step)
    for step in far:
        got_part(1, step)

    logits = logits_t[...]
    gates = upright(jax.nn.sigmoid(logits[0:1] - logits[1:2]))
    gates_other = upright(jax.nn.sigmoid(logits[1:2] - logits[0:1]))
    residual = tok[...].astype(jnp.float32)
    for step in [0] + near[:1] + far + near[1:]:
        if step > 0:
            back_copy(step).wait_recv()
        e = peer(step)
        gate = jnp.where(first == e, gates, gates_other)
        residual += gate * jnp.dot(pick[e], back[e], preferred_element_type=jnp.float32)
    encoded = layer_norm(residual, final[...]).astype(jnp.bfloat16)
    mask = jnp.broadcast_to(live, (rows, 128)).astype(jnp.float32).astype(jnp.bfloat16)
    swap_send[:, :width] = encoded
    swap_send[:, width:] = mask
    exchange = remote(swap_send, swap_recv, es_sem, er_sem, {"dec": 1 - core})
    exchange.start()

    load_block.wait()
    kv_core(0, 0, 0).wait_recv()
    for other, step in pieces:
        kv_core(0, other, step).wait_recv()
        kv_core(1, other, step).wait_recv()
    exchange.wait_recv()
    keep = page_ref[0] == core
    kept = jnp.where(
        keep, swap_send[...].astype(jnp.float32), swap_recv[...].astype(jnp.float32)
    )
    rows_kept = kept[:, :width].astype(jnp.bfloat16)
    alive = kept[:, width : width + 1] > 0
    writes = []
    for i in range(kv.shape[1] // tile):
        cols = pl.ds(i * tile, tile)
        total = jnp.dot(rows_kept, wk[:, cols], preferred_element_type=jnp.float32)
        kv[:, cols] = jnp.where(alive, total + bias[:, cols], 0.0).astype(jnp.bfloat16)
        write = pltpu.make_async_copy(kv.at[:, cols], kv_ref.at[0, :, cols], kv_sem.at[i])
        write.start()
        writes.append(write)

    for copy in swap_weights:
        copy.wait_send()
    for step in range(experts):
        forward(step).wait_send()
        part_copy(step).wait_send()
        if step > 0:
            dispatch(step).wait_send()
            back_copy(step).wait_send()
            kv_z(step).wait_send()
        if step in paired:
            kv_x(step).wait_send()
        else:
            kv_z_other(step).wait_send()
    kv_core(0, 0, 0).wait_send()
    for other, step in pieces:
        kv_y(other, step).wait_send()
        kv_core(0, other, step).wait_send()
        kv_core(1, other, step).wait_send()
    exchange.wait_send()
    for write in writes:
        write.wait()


def kernel_shards(
    capacity,
    tokens,
    expert_ids,
    gate_logits,
    source_lengths,
    page_table,
    norm_gain,
    final_gain,
    w_in,
    w_out,
    w_kv,
    b_kv,
):
    rows, width = tokens.shape
    unit = w_in.shape[2]
    columns = w_kv.shape[1]
    experts = lax.axis_size("exp") // 2
    bf16 = jnp.bfloat16
    block = (experts, capacity, width)
    dma = pltpu.SemaphoreType.DMA
    scalar = pl.BlockSpec(memory_space=pltpu.SMEM)
    anywhere = pl.BlockSpec(memory_space=pl.ANY)
    return pl.pallas_call(
        functools.partial(fused_kernel, experts, capacity),
        out_shape=jax.ShapeDtypeStruct((1, rows, columns), bf16),
        in_specs=[anywhere] * 3 + [scalar] * 2 + [anywhere] * 6,
        out_specs=anywhere,
        scratch_shapes=[
            pltpu.VMEM((rows, width), bf16),
            pltpu.VMEM((2, rows), jnp.int32),
            pltpu.VMEM((2, rows), jnp.float32),
            pltpu.VMEM((1, width), jnp.float32),
            pltpu.VMEM((1, width), jnp.float32),
            pltpu.VMEM((1, columns), jnp.float32),
            pltpu.VMEM((rows, columns), bf16),
            pltpu.VMEM((width, columns), bf16),
            pltpu.VMEM((2,) + w_in.shape[1:], bf16),
            pltpu.VMEM((2,) + w_out.shape[1:], bf16),
            pltpu.VMEM((experts, rows, capacity), bf16),
            pltpu.VMEM(block, bf16),
            pltpu.VMEM((2,) + block, bf16),
            pltpu.VMEM((2, capacity, unit), bf16),
            pltpu.VMEM(block, jnp.float32),
            pltpu.VMEM(block, bf16),
            pltpu.VMEM(block, bf16),
            pltpu.VMEM(block, bf16),
            pltpu.VMEM(block, bf16),
            pltpu.VMEM((rows, width + 128), bf16),
            pltpu.VMEM((rows, width + 128), bf16),
            dma((2,)),
            dma((2,)),
            dma((2,)),
        ]
        + [dma((experts,)) for _ in range(8)]
        + [dma, dma, dma((6,)), dma]
        + [dma((experts,)) for _ in range(6)]
        + [dma((2 * experts,)) for _ in range(2)]
        + [dma((4 * experts,)) for _ in range(2)]
        + [dma((columns // 512,))],
        compiler_params=pltpu.CompilerParams(
            collective_id=0, has_side_effects=True, vmem_limit_bytes=60 * 1024 * 1024
        ),
        cost_estimate=pl.CostEstimate(
            flops=8 * experts * capacity * width * unit * 2,
            bytes_accessed=16 * 1024 * 1024,
            transcendentals=0,
        ),
        name="expert_layer",
    )(
        tokens,
        expert_ids.T,
        gate_logits.T,
        source_lengths,
        page_table,
        norm_gain.reshape(1, width),
        final_gain.reshape(1, width),
        w_in,
        w_out,
        w_kv,
        b_kv.reshape(1, columns),
    )


def any_shards(*args):
    tok_rows = args[0].shape[0]
    experts = lax.axis_size("exp") // 2
    capacity = 2 * max(1, (3 * tok_rows + experts - 1) // (2 * experts))
    whole_tiles = capacity % 16 == 0 and args[9].shape[0] % 32 == 0
    if whole_tiles and experts == 4 and lax.axis_size("dec") == lax.axis_size("rep") == 2:
        return kernel_shards(capacity, *args)
    return shards(*args)


def solution(mesh):
    return jax.shard_map(
        any_shards,
        mesh=mesh,
        in_specs=(
            P(("rep", "exp", "dec"), None),
            P(("rep", "exp", "dec"), None),
            P(("rep", "exp", "dec"), None),
            P(("rep", "exp", "dec")),
            P(("rep", "exp", "dec")),
            P(),
            P(),
            P("exp", None, "dec"),
            P("exp", "dec", None),
            P(("exp", "dec"), None),
            P(),
        ),
        out_specs=P(("rep", "exp", "dec"), None, None),
        check_vma=False,
    )
```

```python
import functools

import jax
import jax.numpy as jnp
from jax import lax
from jax.experimental import pallas as pl
from jax.experimental.pallas import tpu as pltpu
from jax.sharding import PartitionSpec as P

epsilon = 1e-05
MESH = pl.DeviceIdType.MESH


def partner(value, axis, bit):
    mask = 2**bit
    pairs = [(source, source ^ mask) for source in range(lax.axis_size(axis))]
    return lax.ppermute(value, axis, pairs)


def layer_norm(values, scale_gain):
    values = values.astype(jnp.float32)
    center = values - jnp.mean(values, axis=-1, keepdims=True)
    spread = jnp.mean(center * center, axis=-1, keepdims=True)
    return center * lax.rsqrt(spread + epsilon) * scale_gain


def route_slots(expert_ids, is_valid, experts):
    pair_ids = expert_ids.reshape(-1)
    pair_live = jnp.repeat(is_valid, 2)
    onehot = (
        (pair_ids[:, None] == jnp.arange(experts, dtype=jnp.int32)[None, :]) & pair_live[:, None]
    ).astype(jnp.int32)
    before = jnp.cumsum(onehot, axis=0) - onehot
    pair_slots = jnp.sum(before * onehot, axis=1)
    return (pair_ids, pair_live, pair_slots)


def shards(
    tokens,
    expert_ids,
    gate_logits,
    source_lengths,
    page_table,
    norm_gain,
    final_gain,
    w_in,
    w_out,
    w_kv,
    b_kv,
):
    tok_rows, feature_width = tokens.shape
    experts = lax.axis_size("exp") // 2
    capacity = 2 * max(1, (3 * tok_rows + experts - 1) // (2 * experts))
    half_cap = capacity // 2
    position = jnp.arange(tok_rows, dtype=jnp.int32)
    is_valid = position < source_lengths[0]
    normed = layer_norm(tokens, norm_gain).astype(jnp.bfloat16)
    pair_ids, pair_live, pair_slots = route_slots(expert_ids, is_valid, experts)
    overflow_row = experts * capacity
    target = jnp.where(pair_live, pair_ids * capacity + pair_slots, overflow_row)
    outgoing = (
        jnp.zeros((overflow_row, feature_width), jnp.bfloat16)
        .at[target]
        .set(jnp.repeat(normed, 2, axis=0), mode="drop")
    )
    arrived = lax.all_to_all(
        outgoing.reshape(2 * experts, half_cap, feature_width),
        "exp",
        split_axis=0,
        concat_axis=0,
        tiled=True,
    )
    partner_in, partner_out = partner((w_in, w_out), "exp", 0)
    w_inner = jnp.concatenate([w_in[0], partner_in[0]], axis=1)
    w_outer = jnp.concatenate([w_out[0], partner_out[0]], axis=0)
    local_rows = arrived[None]
    block_piece = lax.all_gather(local_rows[None], "dec", axis=0, tiled=True)
    flat_rows = block_piece.reshape(-1, feature_width)
    hidden = jnp.maximum(
        jnp.dot(flat_rows, w_inner, preferred_element_type=jnp.float32), 0.0
    ).astype(jnp.bfloat16)
    partial_out = jnp.dot(hidden, w_outer, preferred_element_type=jnp.float32).reshape(
        block_piece.shape
    )
    summed = partial_out[:, 0]
    reduced = lax.psum_scatter(summed, "dec", scatter_dimension=0, tiled=True)[0].astype(
        jnp.bfloat16
    )
    returned = lax.all_to_all(reduced, "exp", split_axis=0, concat_axis=0, tiled=True).reshape(
        overflow_row, feature_width
    )
    picked = (
        returned[jnp.minimum(target, overflow_row - 1)]
        .astype(jnp.float32)
        .reshape(tok_rows, 2, feature_width)
    )
    gate_weights = jax.nn.sigmoid(gate_logits - gate_logits[:, ::-1])
    mixed_out = jnp.sum(gate_weights[:, :, None] * picked, axis=1)
    residual_sum = tokens.astype(jnp.float32) + jnp.where(is_valid[:, None], mixed_out, 0.0)
    encoded = layer_norm(residual_sum, final_gain).astype(jnp.bfloat16)
    my_core = lax.axis_index("dec")
    keep_own = page_table[0] == my_core
    page_length = source_lengths[0]
    projected = jnp.dot(
        encoded,
        lax.all_gather(w_kv, ("exp", "dec"), axis=0, tiled=True),
        preferred_element_type=jnp.float32,
    )
    keys_values = jnp.where((position < page_length)[:, None], projected + b_kv, 0.0).astype(
        jnp.bfloat16
    )
    page_result = jnp.where(keep_own, keys_values, partner(keys_values, "dec", 0))
    return page_result[None]


def fused_kernel(
    experts,
    capacity,
    tokens_ref,
    ids_ref,
    logits_ref,
    length_ref,
    page_ref,
    norm_ref,
    final_ref,
    w_in_ref,
    w_out_ref,
    w_kv_ref,
    b_kv_ref,
    kv_ref,
    tok,
    ids_t,
    logits_t,
    norm,
    final,
    bias,
    kv,
    wk,
    wi,
    wo,
    pick,
    sends,
    held,
    hid,
    own_sum,
    part_send,
    part_recv,
    back_send,
    back,
    swap_send,
    swap_recv,
    wl_sem,
    ws_sem,
    wr_sem,
    zs_sem,
    zr_sem,
    xs_sem,
    xr_sem,
    ps_sem,
    pr_sem,
    bs_sem,
    br_sem,
    es_sem,
    er_sem,
    in_sem,
    kl_sem,
    zks_sem,
    zkr_sem,
    zls_sem,
    zlr_sem,
    xks_sem,
    xkr_sem,
    yks_sem,
    ykr_sem,
    dks_sem,
    dkr_sem,
    kv_sem,
):
    rows, width = tokens_ref.shape
    group = lax.axis_index("exp")
    part = lax.axis_index("rep")
    core = lax.axis_index("dec")
    z = group // 2
    side = group % 2
    across = 2 * z + (1 - side)

    def peer(step):
        other, bit = 0, 1
        while bit < experts:
            mine, flip = (z // bit) % 2, (step // bit) % 2
            other = other + bit * (mine + flip - 2 * mine * flip)
            bit *= 2
        return other

    inputs = [
        pltpu.make_async_copy(src, dst, in_sem.at[i])
        for i, (src, dst) in enumerate(
            (
                (tokens_ref, tok),
                (ids_ref, ids_t),
                (logits_ref, logits_t),
                (norm_ref, norm),
                (final_ref, final),
                (b_kv_ref, bias),
            )
        )
    ]
    for copy in inputs:
        copy.start()

    barrier = pltpu.get_barrier_semaphore()
    pl.semaphore_signal(barrier, inc=1, device_id={"dec": 1 - core}, device_id_type=MESH)
    pl.semaphore_signal(barrier, inc=1, device_id={"exp": across}, device_id_type=MESH)
    pl.semaphore_signal(barrier, inc=1, device_id={"rep": 1 - part}, device_id_type=MESH)
    for step in range(1, experts):
        pl.semaphore_signal(
            barrier, inc=1, device_id={"exp": 2 * peer(step) + side}, device_id_type=MESH
        )

    local_weights = [
        pltpu.make_async_copy(w_in_ref.at[0], wi.at[0], wl_sem.at[0]),
        pltpu.make_async_copy(w_out_ref.at[0], wo.at[0], wl_sem.at[1]),
    ]
    for copy in local_weights:
        copy.start()

    for copy in inputs:
        copy.wait()
    normed = layer_norm(tok[...], norm[...]).astype(jnp.bfloat16)
    row = lax.broadcasted_iota(jnp.int32, (rows, rows), 0)
    column = lax.broadcasted_iota(jnp.int32, (rows, rows), 1)

    def upright(line):
        return jnp.sum(jnp.where(row == column, line, 0.0), axis=1, keepdims=True)

    ids_f = ids_t[...].astype(jnp.float32)
    first, second = (upright(ids_f[k : k + 1]).astype(jnp.int32) for k in range(2))
    live = lax.broadcasted_iota(jnp.int32, (rows, 1), 0) < length_ref[0]
    lane = lax.broadcasted_iota(jnp.int32, (rows, 128), 1)
    named = ((first == lane) | (second == lane)) & live
    earlier = column < row
    count = jnp.dot(
        earlier.astype(jnp.float32).astype(jnp.bfloat16),
        named.astype(jnp.float32).astype(jnp.bfloat16),
        preferred_element_type=jnp.float32,
    ).astype(jnp.int32)
    slots = jnp.where(named, count, -1)
    slot_lane = lax.broadcasted_iota(jnp.int32, (rows, capacity), 1)
    pl.semaphore_wait(barrier, experts + 2)

    def remote(src, dst, send_sem, recv_sem, where):
        return pltpu.make_async_remote_copy(
            src_ref=src,
            dst_ref=dst,
            send_sem=send_sem,
            recv_sem=recv_sem,
            device_id=where,
            device_id_type=MESH,
        )

    def dispatch(step):
        to = peer(step)
        return remote(
            sends.at[to],
            held.at[0, z],
            zs_sem.at[step],
            zr_sem.at[step],
            {"exp": 2 * to + side},
        )

    block_rows = w_kv_ref.shape[0]
    half_rows = block_rows // 2

    def block(at, column_side, half):
        start = ((2 * at + column_side) * 2 + core) * block_rows + half * half_rows
        return wk.at[pl.ds(pl.multiple_of(start, half_rows), half_rows)]

    own_start = pl.multiple_of((2 * group + core) * block_rows, block_rows)
    own_block = wk.at[pl.ds(own_start, block_rows)]
    own_half = w_kv_ref.at[pl.ds(pl.multiple_of(part * half_rows, half_rows), half_rows)]
    load_block = pltpu.make_async_copy(w_kv_ref, own_block, kl_sem)

    def kv_z(step):
        where = {"exp": 2 * peer(step) + side}
        return remote(
            own_half, block(z, side, part), zks_sem.at[step], zkr_sem.at[step], where
        )

    def kv_z_other(step):
        where = {"exp": 2 * peer(step) + side}
        piece = block(z, 1 - side, part)
        return remote(piece, piece, zls_sem.at[step], zlr_sem.at[step], where)

    def kv_x(step):
        piece = block(peer(step), side, part)
        source = own_half if step == 0 else piece
        return remote(source, piece, xks_sem.at[step], xkr_sem.at[step], {"exp": across})

    def kv_y(other, step):
        piece = block(peer(step), 1 - side if other else side, part)
        index = other * experts + step
        return remote(
            piece, piece, yks_sem.at[index], ykr_sem.at[index], {"rep": 1 - part}
        )

    def kv_core(late, other, step):
        index = (late * 2 + other) * experts + step
        where = {"dec": 1 - core}
        if other == 0 and step == 0:
            return remote(w_kv_ref, own_block, dks_sem.at[index], dkr_sem.at[index], where)
        half = 1 - part if late else part
        piece = block(peer(step), 1 - side if other else side, half)
        return remote(piece, piece, dks_sem.at[index], dkr_sem.at[index], where)

    pieces = [(0, step) for step in range(1, experts)] + [(1, step) for step in range(experts)]
    paired = [step for step in range(experts) if step % 2 == 0]
    unpaired = [step for step in range(experts) if step % 2 == 1]

    def got_own(step):
        kv_z(step).wait_recv()
        if step in paired:
            kv_x(step).start()
        kv_y(0, step).start()
        kv_core(0, 0, step).start()

    def got_other(step):
        if step in paired:
            kv_x(step).wait_recv()
        else:
            kv_z_other(step).wait_recv()
        if step == 0:
            for towards in unpaired:
                kv_z_other(towards).start()
        kv_y(1, step).start()
        kv_core(0, 1, step).start()

    def got_part(other, step):
        kv_y(other, step).wait_recv()
        kv_core(1, other, step).start()

    swap_weights = [
        remote(w_in_ref.at[0], wi.at[1], ws_sem.at[0], wr_sem.at[0], {"dec": 1 - core}),
        remote(w_out_ref.at[0], wo.at[1], ws_sem.at[1], wr_sem.at[1], {"dec": 1 - core}),
    ]

    def forward(step):
        at = peer(step)
        return remote(
            held.at[0, at], held.at[1, at], xs_sem.at[step], xr_sem.at[step], {"exp": across}
        )

    slab = capacity // 2

    def part_copy(step, half):
        lines = pl.ds(half * slab, slab)
        return remote(
            part_send.at[step, lines],
            part_recv.at[step, lines],
            ps_sem.at[half * experts + step],
            pr_sem.at[half * experts + step],
            {"exp": across},
        )

    def back_copy(step, half):
        lines = pl.ds(half * slab, slab)
        return remote(
            back_send.at[step, lines],
            back.at[z, lines],
            bs_sem.at[half * experts + step],
            br_sem.at[half * experts + step],
            {"exp": 2 * peer(step) + side},
        )

    unit = wi.shape[2]
    tile = 512

    def ffn(column, at, store):
        def inner(i, carry):
            half = i // (unit // tile)
            offset = pl.multiple_of(i % (unit // tile) * tile, tile)
            block = jnp.dot(
                held[column, at],
                wi[half, :, pl.ds(offset, tile)],
                preferred_element_type=jnp.float32,
            )
            hid[half, :, pl.ds(offset, tile)] = jnp.maximum(block, 0.0).astype(jnp.bfloat16)
            return carry

        lax.fori_loop(0, 2 * (unit // tile), inner, 0)

        def outer(i, carry):
            cols = pl.ds(pl.multiple_of(i * tile, tile), tile)
            total = jnp.dot(hid[0], wo[0, :, cols], preferred_element_type=jnp.float32)
            total += jnp.dot(hid[1], wo[1, :, cols], preferred_element_type=jnp.float32)
            store(cols, total)
            return carry

        lax.fori_loop(0, width // tile, outer, 0)

    def ffn_own(step):
        def store(cols, total):
            own_sum[step, :, cols] = total

        ffn(0, peer(step), store)

    def ffn_other(step):
        def store(cols, total):
            part_send[step, :, cols] = total.astype(jnp.bfloat16)

        ffn(1, peer(step), store)
        for half in range(2):
            part_copy(step, half).start()

    def finish(step):
        for half in range(2):
            lines = pl.ds(half * slab, slab)
            part_copy(step, half).wait_recv()
            total = own_sum[step, lines] + part_recv[step, lines].astype(jnp.float32)
            if step == 0:
                back[z, lines] = total.astype(jnp.bfloat16)
            else:
                back_send[step, lines] = total.astype(jnp.bfloat16)
                back_copy(step, half).start()

    for copy in swap_weights:
        copy.start()
    near, far = unpaired, paired[1:]
    for step in near + [0] + far:
        e = peer(step)
        slot = jnp.sum(jnp.where(lane == e, slots, 0), axis=1, keepdims=True)
        chosen = (slot == slot_lane).astype(jnp.float32).astype(jnp.bfloat16)
        pick[e] = chosen
        gathered = lax.dot_general(
            chosen, normed, (((0,), (0,)), ((), ())), preferred_element_type=jnp.float32
        ).astype(jnp.bfloat16)
        if step == 0:
            held[0, z] = gathered
            forward(0).start()
        else:
            sends[e] = gathered
            dispatch(step).start()
    kv_x(0).start()
    for step in near + far:
        kv_z(step).start()
    load_block.start()
    kv_core(0, 0, 0).start()
    for copy in local_weights:
        copy.wait()
    for copy in swap_weights:
        copy.wait_recv()
    ffn_own(0)
    for step in near:
        dispatch(step).wait_recv()
        forward(step).start()
        if step == near[0]:
            forward(0).wait_recv()
            ffn_other(0)
    got_other(0)
    got_own(near[0])
    ffn_own(near[0])
    for step in far:
        dispatch(step).wait_recv()
        forward(step).start()
    forward(near[0]).wait_recv()
    ffn_other(near[0])
    for step in near[1:] + far:
        got_own(step)
        ffn_own(step)
    finish(0)
    for step in far + near[1:]:
        forward(step).wait_recv()
        ffn_other(step)
    got_part(1, 0)
    for step in near:
        got_other(step)
    finish(near[0])
    for step in near:
        got_part(0, step)
    for step in far:
        got_other(step)
    for step in far + near[1:]:
        finish(step)
    for step in near:
        got_part(1, step)
    for step in far:
        got_part(0, step)
    for step in far:
        got_part(1, step)

    logits = logits_t[...]
    gates = upright(jax.nn.sigmoid(logits[0:1] - logits[1:2]))
    gates_other = upright(jax.nn.sigmoid(logits[1:2] - logits[0:1]))
    residual = tok[...].astype(jnp.float32)
    for step in [0] + near[:1] + far + near[1:]:
        if step > 0:
            for half in range(2):
                back_copy(step, half).wait_recv()
        e = peer(step)
        gate = jnp.where(first == e, gates, gates_other)
        residual += gate * jnp.dot(pick[e], back[e], preferred_element_type=jnp.float32)
    encoded = layer_norm(residual, final[...]).astype(jnp.bfloat16)
    mask = jnp.broadcast_to(live, (rows, 128)).astype(jnp.float32).astype(jnp.bfloat16)
    swap_send[:, :width] = encoded
    swap_send[:, width:] = mask
    exchange = remote(swap_send, swap_recv, es_sem, er_sem, {"dec": 1 - core})
    exchange.start()

    load_block.wait()
    kv_core(0, 0, 0).wait_recv()
    for other, step in pieces:
        kv_core(0, other, step).wait_recv()
        kv_core(1, other, step).wait_recv()
    exchange.wait_recv()
    keep = page_ref[0] == core
    kept = jnp.where(
        keep, swap_send[...].astype(jnp.float32), swap_recv[...].astype(jnp.float32)
    )
    rows_kept = kept[:, :width].astype(jnp.bfloat16)
    alive = kept[:, width : width + 1] > 0
    writes = []
    for i in range(kv.shape[1] // tile):
        cols = pl.ds(i * tile, tile)
        total = jnp.dot(rows_kept, wk[:, cols], preferred_element_type=jnp.float32)
        kv[:, cols] = jnp.where(alive, total + bias[:, cols], 0.0).astype(jnp.bfloat16)
        write = pltpu.make_async_copy(kv.at[:, cols], kv_ref.at[0, :, cols], kv_sem.at[i])
        write.start()
        writes.append(write)

    for copy in swap_weights:
        copy.wait_send()
    for step in range(experts):
        forward(step).wait_send()
        for half in range(2):
            part_copy(step, half).wait_send()
            if step > 0:
                back_copy(step, half).wait_send()
        if step > 0:
            dispatch(step).wait_send()
            kv_z(step).wait_send()
        if step in paired:
            kv_x(step).wait_send()
        else:
            kv_z_other(step).wait_send()
    kv_core(0, 0, 0).wait_send()
    for other, step in pieces:
        kv_y(other, step).wait_send()
        kv_core(0, other, step).wait_send()
        kv_core(1, other, step).wait_send()
    exchange.wait_send()
    for write in writes:
        write.wait()


def kernel_shards(
    capacity,
    tokens,
    expert_ids,
    gate_logits,
    source_lengths,
    page_table,
    norm_gain,
    final_gain,
    w_in,
    w_out,
    w_kv,
    b_kv,
):
    rows, width = tokens.shape
    unit = w_in.shape[2]
    columns = w_kv.shape[1]
    experts = lax.axis_size("exp") // 2
    bf16 = jnp.bfloat16
    block = (experts, capacity, width)
    dma = pltpu.SemaphoreType.DMA
    scalar = pl.BlockSpec(memory_space=pltpu.SMEM)
    anywhere = pl.BlockSpec(memory_space=pl.ANY)
    return pl.pallas_call(
        functools.partial(fused_kernel, experts, capacity),
        out_shape=jax.ShapeDtypeStruct((1, rows, columns), bf16),
        in_specs=[anywhere] * 3 + [scalar] * 2 + [anywhere] * 6,
        out_specs=anywhere,
        scratch_shapes=[
            pltpu.VMEM((rows, width), bf16),
            pltpu.VMEM((2, rows), jnp.int32),
            pltpu.VMEM((2, rows), jnp.float32),
            pltpu.VMEM((1, width), jnp.float32),
            pltpu.VMEM((1, width), jnp.float32),
            pltpu.VMEM((1, columns), jnp.float32),
            pltpu.VMEM((rows, columns), bf16),
            pltpu.VMEM((width, columns), bf16),
            pltpu.VMEM((2,) + w_in.shape[1:], bf16),
            pltpu.VMEM((2,) + w_out.shape[1:], bf16),
            pltpu.VMEM((experts, rows, capacity), bf16),
            pltpu.VMEM(block, bf16),
            pltpu.VMEM((2,) + block, bf16),
            pltpu.VMEM((2, capacity, unit), bf16),
            pltpu.VMEM(block, jnp.float32),
            pltpu.VMEM(block, bf16),
            pltpu.VMEM(block, bf16),
            pltpu.VMEM(block, bf16),
            pltpu.VMEM(block, bf16),
            pltpu.VMEM((rows, width + 128), bf16),
            pltpu.VMEM((rows, width + 128), bf16),
            dma((2,)),
            dma((2,)),
            dma((2,)),
        ]
        + [dma((experts,)) for _ in range(4)]
        + [dma((2 * experts,)) for _ in range(4)]
        + [dma, dma, dma((6,)), dma]
        + [dma((experts,)) for _ in range(6)]
        + [dma((2 * experts,)) for _ in range(2)]
        + [dma((4 * experts,)) for _ in range(2)]
        + [dma((columns // 512,))],
        compiler_params=pltpu.CompilerParams(
            collective_id=0, has_side_effects=True, vmem_limit_bytes=60 * 1024 * 1024
        ),
        cost_estimate=pl.CostEstimate(
            flops=8 * experts * capacity * width * unit * 2,
            bytes_accessed=16 * 1024 * 1024,
            transcendentals=0,
        ),
        name="expert_layer",
    )(
        tokens,
        expert_ids.T,
        gate_logits.T,
        source_lengths,
        page_table,
        norm_gain.reshape(1, width),
        final_gain.reshape(1, width),
        w_in,
        w_out,
        w_kv,
        b_kv.reshape(1, columns),
    )


def any_shards(*args):
    tok_rows = args[0].shape[0]
    experts = lax.axis_size("exp") // 2
    capacity = 2 * max(1, (3 * tok_rows + experts - 1) // (2 * experts))
    whole_tiles = capacity % 32 == 0 and args[9].shape[0] % 32 == 0
    if whole_tiles and experts == 4 and lax.axis_size("dec") == lax.axis_size("rep") == 2:
        return kernel_shards(capacity, *args)
    return shards(*args)


def solution(mesh):
    return jax.shard_map(
        any_shards,
        mesh=mesh,
        in_specs=(
            P(("rep", "exp", "dec"), None),
            P(("rep", "exp", "dec"), None),
            P(("rep", "exp", "dec"), None),
            P(("rep", "exp", "dec")),
            P(("rep", "exp", "dec")),
            P(),
            P(),
            P("exp", None, "dec"),
            P("exp", "dec", None),
            P(("exp", "dec"), None),
            P(),
        ),
        out_specs=P(("rep", "exp", "dec"), None, None),
        check_vma=False,
    )
```

```python
import functools

import jax
import jax.numpy as jnp
from jax import lax
from jax.experimental import pallas as pl
from jax.experimental.pallas import tpu as pltpu
from jax.sharding import PartitionSpec as P

epsilon = 1e-05
MESH = pl.DeviceIdType.MESH


def partner(value, axis, bit):
    mask = 2**bit
    pairs = [(source, source ^ mask) for source in range(lax.axis_size(axis))]
    return lax.ppermute(value, axis, pairs)


def layer_norm(values, scale_gain):
    values = values.astype(jnp.float32)
    center = values - jnp.mean(values, axis=-1, keepdims=True)
    spread = jnp.mean(center * center, axis=-1, keepdims=True)
    return center * lax.rsqrt(spread + epsilon) * scale_gain


def route_slots(expert_ids, is_valid, experts):
    pair_ids = expert_ids.reshape(-1)
    pair_live = jnp.repeat(is_valid, 2)
    onehot = (
        (pair_ids[:, None] == jnp.arange(experts, dtype=jnp.int32)[None, :]) & pair_live[:, None]
    ).astype(jnp.int32)
    before = jnp.cumsum(onehot, axis=0) - onehot
    pair_slots = jnp.sum(before * onehot, axis=1)
    return (pair_ids, pair_live, pair_slots)


def shards(
    tokens,
    expert_ids,
    gate_logits,
    source_lengths,
    page_table,
    norm_gain,
    final_gain,
    w_in,
    w_out,
    w_kv,
    b_kv,
):
    tok_rows, feature_width = tokens.shape
    experts = lax.axis_size("exp") // 2
    capacity = 2 * max(1, (3 * tok_rows + experts - 1) // (2 * experts))
    half_cap = capacity // 2
    position = jnp.arange(tok_rows, dtype=jnp.int32)
    is_valid = position < source_lengths[0]
    normed = layer_norm(tokens, norm_gain).astype(jnp.bfloat16)
    pair_ids, pair_live, pair_slots = route_slots(expert_ids, is_valid, experts)
    overflow_row = experts * capacity
    target = jnp.where(pair_live, pair_ids * capacity + pair_slots, overflow_row)
    outgoing = (
        jnp.zeros((overflow_row, feature_width), jnp.bfloat16)
        .at[target]
        .set(jnp.repeat(normed, 2, axis=0), mode="drop")
    )
    arrived = lax.all_to_all(
        outgoing.reshape(2 * experts, half_cap, feature_width),
        "exp",
        split_axis=0,
        concat_axis=0,
        tiled=True,
    )
    partner_in, partner_out = partner((w_in, w_out), "exp", 0)
    w_inner = jnp.concatenate([w_in[0], partner_in[0]], axis=1)
    w_outer = jnp.concatenate([w_out[0], partner_out[0]], axis=0)
    local_rows = arrived[None]
    block_piece = lax.all_gather(local_rows[None], "dec", axis=0, tiled=True)
    flat_rows = block_piece.reshape(-1, feature_width)
    hidden = jnp.maximum(
        jnp.dot(flat_rows, w_inner, preferred_element_type=jnp.float32), 0.0
    ).astype(jnp.bfloat16)
    partial_out = jnp.dot(hidden, w_outer, preferred_element_type=jnp.float32).reshape(
        block_piece.shape
    )
    summed = partial_out[:, 0]
    reduced = lax.psum_scatter(summed, "dec", scatter_dimension=0, tiled=True)[0].astype(
        jnp.bfloat16
    )
    returned = lax.all_to_all(reduced, "exp", split_axis=0, concat_axis=0, tiled=True).reshape(
        overflow_row, feature_width
    )
    picked = (
        returned[jnp.minimum(target, overflow_row - 1)]
        .astype(jnp.float32)
        .reshape(tok_rows, 2, feature_width)
    )
    gate_weights = jax.nn.sigmoid(gate_logits - gate_logits[:, ::-1])
    mixed_out = jnp.sum(gate_weights[:, :, None] * picked, axis=1)
    residual_sum = tokens.astype(jnp.float32) + jnp.where(is_valid[:, None], mixed_out, 0.0)
    encoded = layer_norm(residual_sum, final_gain).astype(jnp.bfloat16)
    my_core = lax.axis_index("dec")
    keep_own = page_table[0] == my_core
    page_length = source_lengths[0]
    projected = jnp.dot(
        encoded,
        lax.all_gather(w_kv, ("exp", "dec"), axis=0, tiled=True),
        preferred_element_type=jnp.float32,
    )
    keys_values = jnp.where((position < page_length)[:, None], projected + b_kv, 0.0).astype(
        jnp.bfloat16
    )
    page_result = jnp.where(keep_own, keys_values, partner(keys_values, "dec", 0))
    return page_result[None]


def fused_kernel(
    experts,
    capacity,
    tokens_ref,
    ids_ref,
    logits_ref,
    length_ref,
    page_ref,
    norm_ref,
    final_ref,
    w_in_ref,
    w_out_ref,
    w_kv_ref,
    b_kv_ref,
    kv_ref,
    tok,
    ids_t,
    logits_t,
    norm,
    final,
    bias,
    kv,
    wk,
    wi,
    wo,
    pick,
    sends,
    held,
    hid,
    own_sum,
    part_send,
    part_recv,
    back_send,
    back,
    swap_send,
    swap_recv,
    wl_sem,
    ws_sem,
    wr_sem,
    zs_sem,
    zr_sem,
    xs_sem,
    xr_sem,
    ps_sem,
    pr_sem,
    bs_sem,
    br_sem,
    es_sem,
    er_sem,
    in_sem,
    kl_sem,
    zks_sem,
    zkr_sem,
    zls_sem,
    zlr_sem,
    xks_sem,
    xkr_sem,
    yks_sem,
    ykr_sem,
    dks_sem,
    dkr_sem,
    kv_sem,
):
    rows, width = tokens_ref.shape
    group = lax.axis_index("exp")
    part = lax.axis_index("rep")
    core = lax.axis_index("dec")
    z = group // 2
    side = group % 2
    across = 2 * z + (1 - side)

    def peer(step):
        other, bit = 0, 1
        while bit < experts:
            mine, flip = (z // bit) % 2, (step // bit) % 2
            other = other + bit * (mine + flip - 2 * mine * flip)
            bit *= 2
        return other

    inputs = [
        pltpu.make_async_copy(src, dst, in_sem.at[i])
        for i, (src, dst) in enumerate(
            (
                (tokens_ref, tok),
                (ids_ref, ids_t),
                (logits_ref, logits_t),
                (norm_ref, norm),
                (final_ref, final),
                (b_kv_ref, bias),
            )
        )
    ]
    for copy in inputs:
        copy.start()

    barrier = pltpu.get_barrier_semaphore()
    pl.semaphore_signal(barrier, inc=1, device_id={"dec": 1 - core}, device_id_type=MESH)
    pl.semaphore_signal(barrier, inc=1, device_id={"exp": across}, device_id_type=MESH)
    pl.semaphore_signal(barrier, inc=1, device_id={"rep": 1 - part}, device_id_type=MESH)
    for step in range(1, experts):
        pl.semaphore_signal(
            barrier, inc=1, device_id={"exp": 2 * peer(step) + side}, device_id_type=MESH
        )

    local_weights = [
        pltpu.make_async_copy(w_in_ref.at[0], wi.at[0], wl_sem.at[0]),
        pltpu.make_async_copy(w_out_ref.at[0], wo.at[0], wl_sem.at[1]),
    ]
    for copy in local_weights:
        copy.start()

    for copy in inputs:
        copy.wait()
    normed = layer_norm(tok[...], norm[...]).astype(jnp.bfloat16)
    row = lax.broadcasted_iota(jnp.int32, (rows, rows), 0)
    column = lax.broadcasted_iota(jnp.int32, (rows, rows), 1)

    def upright(line):
        return jnp.sum(jnp.where(row == column, line, 0.0), axis=1, keepdims=True)

    ids_f = ids_t[...].astype(jnp.float32)
    first, second = (upright(ids_f[k : k + 1]).astype(jnp.int32) for k in range(2))
    live = lax.broadcasted_iota(jnp.int32, (rows, 1), 0) < length_ref[0]
    lane = lax.broadcasted_iota(jnp.int32, (rows, 128), 1)
    named = ((first == lane) | (second == lane)) & live
    earlier = column < row
    count = jnp.dot(
        earlier.astype(jnp.float32).astype(jnp.bfloat16),
        named.astype(jnp.float32).astype(jnp.bfloat16),
        preferred_element_type=jnp.float32,
    ).astype(jnp.int32)
    slots = jnp.where(named, count, -1)
    slot_lane = lax.broadcasted_iota(jnp.int32, (rows, capacity), 1)
    pl.semaphore_wait(barrier, experts + 2)

    def remote(src, dst, send_sem, recv_sem, where):
        return pltpu.make_async_remote_copy(
            src_ref=src,
            dst_ref=dst,
            send_sem=send_sem,
            recv_sem=recv_sem,
            device_id=where,
            device_id_type=MESH,
        )

    def dispatch(step):
        to = peer(step)
        return remote(
            sends.at[to],
            held.at[0, z],
            zs_sem.at[step],
            zr_sem.at[step],
            {"exp": 2 * to + side},
        )

    block_rows = w_kv_ref.shape[0]
    half_rows = block_rows // 2

    def block(at, column_side, half):
        start = ((2 * at + column_side) * 2 + core) * block_rows + half * half_rows
        return wk.at[pl.ds(pl.multiple_of(start, half_rows), half_rows)]

    own_start = pl.multiple_of((2 * group + core) * block_rows, block_rows)
    own_block = wk.at[pl.ds(own_start, block_rows)]
    own_half = w_kv_ref.at[pl.ds(pl.multiple_of(part * half_rows, half_rows), half_rows)]
    load_block = pltpu.make_async_copy(w_kv_ref, own_block, kl_sem)

    def kv_z(step):
        where = {"exp": 2 * peer(step) + side}
        return remote(
            own_half, block(z, side, part), zks_sem.at[step], zkr_sem.at[step], where
        )

    def kv_z_other(step):
        where = {"exp": 2 * peer(step) + side}
        piece = block(z, 1 - side, part)
        return remote(piece, piece, zls_sem.at[step], zlr_sem.at[step], where)

    def kv_x(step):
        piece = block(peer(step), side, part)
        source = own_half if step == 0 else piece
        return remote(source, piece, xks_sem.at[step], xkr_sem.at[step], {"exp": across})

    def kv_y(other, step):
        piece = block(peer(step), 1 - side if other else side, part)
        index = other * experts + step
        return remote(
            piece, piece, yks_sem.at[index], ykr_sem.at[index], {"rep": 1 - part}
        )

    def kv_core(late, other, step):
        index = (late * 2 + other) * experts + step
        where = {"dec": 1 - core}
        if other == 0 and step == 0:
            return remote(w_kv_ref, own_block, dks_sem.at[index], dkr_sem.at[index], where)
        half = 1 - part if late else part
        piece = block(peer(step), 1 - side if other else side, half)
        return remote(piece, piece, dks_sem.at[index], dkr_sem.at[index], where)

    pieces = [(0, step) for step in range(1, experts)] + [(1, step) for step in range(experts)]
    paired = [step for step in range(experts) if step % 2 == 0]
    unpaired = [step for step in range(experts) if step % 2 == 1]

    def got_own(step):
        kv_z(step).wait_recv()
        if step in paired:
            kv_x(step).start()
        kv_y(0, step).start()
        kv_core(0, 0, step).start()

    def got_other(step):
        if step in paired:
            kv_x(step).wait_recv()
        else:
            kv_z_other(step).wait_recv()
        if step == 0:
            for towards in unpaired:
                kv_z_other(towards).start()
        kv_y(1, step).start()
        kv_core(0, 1, step).start()

    def got_part(other, step):
        kv_y(other, step).wait_recv()
        kv_core(1, other, step).start()

    swap_weights = [
        remote(w_in_ref.at[0], wi.at[1], ws_sem.at[0], wr_sem.at[0], {"dec": 1 - core}),
        remote(w_out_ref.at[0], wo.at[1], ws_sem.at[1], wr_sem.at[1], {"dec": 1 - core}),
    ]

    def forward(step):
        at = peer(step)
        return remote(
            held.at[0, at], held.at[1, at], xs_sem.at[step], xr_sem.at[step], {"exp": across}
        )

    slab = capacity // 2

    def part_copy(step, half):
        lines = pl.ds(half * slab, slab)
        return remote(
            part_send.at[step, lines],
            part_recv.at[step, lines],
            ps_sem.at[half * experts + step],
            pr_sem.at[half * experts + step],
            {"exp": across},
        )

    def back_copy(step, half):
        lines = pl.ds(half * slab, slab)
        return remote(
            back_send.at[step, lines],
            back.at[z, lines],
            bs_sem.at[half * experts + step],
            br_sem.at[half * experts + step],
            {"exp": 2 * peer(step) + side},
        )

    unit = wi.shape[2]
    tile = 512

    def ffn(column, at, store):
        def inner(i, carry):
            half = i // (unit // tile)
            offset = pl.multiple_of(i % (unit // tile) * tile, tile)
            block = jnp.dot(
                held[column, at],
                wi[half, :, pl.ds(offset, tile)],
                preferred_element_type=jnp.float32,
            )
            hid[half, :, pl.ds(offset, tile)] = jnp.maximum(block, 0.0).astype(jnp.bfloat16)
            return carry

        lax.fori_loop(0, 2 * (unit // tile), inner, 0)

        def outer(i, carry):
            cols = pl.ds(pl.multiple_of(i * tile, tile), tile)
            total = jnp.dot(hid[0], wo[0, :, cols], preferred_element_type=jnp.float32)
            total += jnp.dot(hid[1], wo[1, :, cols], preferred_element_type=jnp.float32)
            store(cols, total)
            return carry

        lax.fori_loop(0, width // tile, outer, 0)

    def ffn_own(step):
        def store(cols, total):
            own_sum[step, :, cols] = total

        ffn(0, peer(step), store)

    def ffn_other(step):
        def store(cols, total):
            part_send[step, :, cols] = total.astype(jnp.bfloat16)

        ffn(1, peer(step), store)
        for half in range(2):
            part_copy(step, half).start()

    def finish(step):
        for half in range(2):
            lines = pl.ds(half * slab, slab)
            part_copy(step, half).wait_recv()
            total = own_sum[step, lines] + part_recv[step, lines].astype(jnp.float32)
            if step == 0:
                back[z, lines] = total.astype(jnp.bfloat16)
            else:
                back_send[step, lines] = total.astype(jnp.bfloat16)
                back_copy(step, half).start()

    for copy in swap_weights:
        copy.start()
    near, far = unpaired, paired[1:]
    for step in near + [0] + far:
        e = peer(step)
        slot = jnp.sum(jnp.where(lane == e, slots, 0), axis=1, keepdims=True)
        chosen = (slot == slot_lane).astype(jnp.float32).astype(jnp.bfloat16)
        pick[e] = chosen
        gathered = lax.dot_general(
            chosen, normed, (((0,), (0,)), ((), ())), preferred_element_type=jnp.float32
        ).astype(jnp.bfloat16)
        if step == 0:
            held[0, z] = gathered
            forward(0).start()
        else:
            sends[e] = gathered
            dispatch(step).start()
    kv_x(0).start()
    for step in near + far:
        kv_z(step).start()
    load_block.start()
    kv_core(0, 0, 0).start()
    for copy in local_weights:
        copy.wait()
    for copy in swap_weights:
        copy.wait_recv()
    ffn_own(0)
    for step in near:
        dispatch(step).wait_recv()
        forward(step).start()
        if step == near[0]:
            forward(0).wait_recv()
            ffn_other(0)
    got_other(0)
    got_own(near[0])
    ffn_own(near[0])
    for step in far:
        dispatch(step).wait_recv()
        forward(step).start()
    forward(near[0]).wait_recv()
    ffn_other(near[0])
    for step in near[1:] + far:
        got_own(step)
        ffn_own(step)
    finish(0)
    for step in far + near[1:]:
        forward(step).wait_recv()
        ffn_other(step)
    got_part(1, 0)
    for step in near:
        got_other(step)
    finish(near[0])
    for step in far:
        finish(step)
        got_other(step)
    for step in near[1:]:
        finish(step)
    for step in near:
        got_part(0, step)
    for step in near:
        got_part(1, step)
    for step in far:
        got_part(0, step)
    for step in far:
        got_part(1, step)

    logits = logits_t[...]
    gates = upright(jax.nn.sigmoid(logits[0:1] - logits[1:2]))
    gates_other = upright(jax.nn.sigmoid(logits[1:2] - logits[0:1]))
    residual = tok[...].astype(jnp.float32)
    for step in [0] + near[:1] + far + near[1:]:
        if step > 0:
            for half in range(2):
                back_copy(step, half).wait_recv()
        e = peer(step)
        gate = jnp.where(first == e, gates, gates_other)
        residual += gate * jnp.dot(pick[e], back[e], preferred_element_type=jnp.float32)
    encoded = layer_norm(residual, final[...]).astype(jnp.bfloat16)
    mask = jnp.broadcast_to(live, (rows, 128)).astype(jnp.float32).astype(jnp.bfloat16)
    swap_send[:, :width] = encoded
    swap_send[:, width:] = mask
    exchange = remote(swap_send, swap_recv, es_sem, er_sem, {"dec": 1 - core})
    exchange.start()

    load_block.wait()
    kv_core(0, 0, 0).wait_recv()
    for other, step in pieces:
        kv_core(0, other, step).wait_recv()
        kv_core(1, other, step).wait_recv()
    exchange.wait_recv()
    keep = page_ref[0] == core
    kept = jnp.where(
        keep, swap_send[...].astype(jnp.float32), swap_recv[...].astype(jnp.float32)
    )
    rows_kept = kept[:, :width].astype(jnp.bfloat16)
    alive = kept[:, width : width + 1] > 0
    writes = []
    for i in range(kv.shape[1] // tile):
        cols = pl.ds(i * tile, tile)
        total = jnp.dot(rows_kept, wk[:, cols], preferred_element_type=jnp.float32)
        kv[:, cols] = jnp.where(alive, total + bias[:, cols], 0.0).astype(jnp.bfloat16)
        write = pltpu.make_async_copy(kv.at[:, cols], kv_ref.at[0, :, cols], kv_sem.at[i])
        write.start()
        writes.append(write)

    for copy in swap_weights:
        copy.wait_send()
    for step in range(experts):
        forward(step).wait_send()
        for half in range(2):
            part_copy(step, half).wait_send()
            if step > 0:
                back_copy(step, half).wait_send()
        if step > 0:
            dispatch(step).wait_send()
            kv_z(step).wait_send()
        if step in paired:
            kv_x(step).wait_send()
        else:
            kv_z_other(step).wait_send()
    kv_core(0, 0, 0).wait_send()
    for other, step in pieces:
        kv_y(other, step).wait_send()
        kv_core(0, other, step).wait_send()
        kv_core(1, other, step).wait_send()
    exchange.wait_send()
    for write in writes:
        write.wait()


def kernel_shards(
    capacity,
    tokens,
    expert_ids,
    gate_logits,
    source_lengths,
    page_table,
    norm_gain,
    final_gain,
    w_in,
    w_out,
    w_kv,
    b_kv,
):
    rows, width = tokens.shape
    unit = w_in.shape[2]
    columns = w_kv.shape[1]
    experts = lax.axis_size("exp") // 2
    bf16 = jnp.bfloat16
    block = (experts, capacity, width)
    dma = pltpu.SemaphoreType.DMA
    scalar = pl.BlockSpec(memory_space=pltpu.SMEM)
    anywhere = pl.BlockSpec(memory_space=pl.ANY)
    return pl.pallas_call(
        functools.partial(fused_kernel, experts, capacity),
        out_shape=jax.ShapeDtypeStruct((1, rows, columns), bf16),
        in_specs=[anywhere] * 3 + [scalar] * 2 + [anywhere] * 6,
        out_specs=anywhere,
        scratch_shapes=[
            pltpu.VMEM((rows, width), bf16),
            pltpu.VMEM((2, rows), jnp.int32),
            pltpu.VMEM((2, rows), jnp.float32),
            pltpu.VMEM((1, width), jnp.float32),
            pltpu.VMEM((1, width), jnp.float32),
            pltpu.VMEM((1, columns), jnp.float32),
            pltpu.VMEM((rows, columns), bf16),
            pltpu.VMEM((width, columns), bf16),
            pltpu.VMEM((2,) + w_in.shape[1:], bf16),
            pltpu.VMEM((2,) + w_out.shape[1:], bf16),
            pltpu.VMEM((experts, rows, capacity), bf16),
            pltpu.VMEM(block, bf16),
            pltpu.VMEM((2,) + block, bf16),
            pltpu.VMEM((2, capacity, unit), bf16),
            pltpu.VMEM(block, jnp.float32),
            pltpu.VMEM(block, bf16),
            pltpu.VMEM(block, bf16),
            pltpu.VMEM(block, bf16),
            pltpu.VMEM(block, bf16),
            pltpu.VMEM((rows, width + 128), bf16),
            pltpu.VMEM((rows, width + 128), bf16),
            dma((2,)),
            dma((2,)),
            dma((2,)),
        ]
        + [dma((experts,)) for _ in range(4)]
        + [dma((2 * experts,)) for _ in range(4)]
        + [dma, dma, dma((6,)), dma]
        + [dma((experts,)) for _ in range(6)]
        + [dma((2 * experts,)) for _ in range(2)]
        + [dma((4 * experts,)) for _ in range(2)]
        + [dma((columns // 512,))],
        compiler_params=pltpu.CompilerParams(
            collective_id=0, has_side_effects=True, vmem_limit_bytes=60 * 1024 * 1024
        ),
        cost_estimate=pl.CostEstimate(
            flops=8 * experts * capacity * width * unit * 2,
            bytes_accessed=16 * 1024 * 1024,
            transcendentals=0,
        ),
        name="expert_layer",
    )(
        tokens,
        expert_ids.T,
        gate_logits.T,
        source_lengths,
        page_table,
        norm_gain.reshape(1, width),
        final_gain.reshape(1, width),
        w_in,
        w_out,
        w_kv,
        b_kv.reshape(1, columns),
    )


def any_shards(*args):
    tok_rows = args[0].shape[0]
    experts = lax.axis_size("exp") // 2
    capacity = 2 * max(1, (3 * tok_rows + experts - 1) // (2 * experts))
    whole_tiles = capacity % 32 == 0 and args[9].shape[0] % 32 == 0
    if whole_tiles and experts == 4 and lax.axis_size("dec") == lax.axis_size("rep") == 2:
        return kernel_shards(capacity, *args)
    return shards(*args)


def solution(mesh):
    return jax.shard_map(
        any_shards,
        mesh=mesh,
        in_specs=(
            P(("rep", "exp", "dec"), None),
            P(("rep", "exp", "dec"), None),
            P(("rep", "exp", "dec"), None),
            P(("rep", "exp", "dec")),
            P(("rep", "exp", "dec")),
            P(),
            P(),
            P("exp", None, "dec"),
            P("exp", "dec", None),
            P(("exp", "dec"), None),
            P(),
        ),
        out_specs=P(("rep", "exp", "dec"), None, None),
        check_vma=False,
    )
```
